32 devices in a mesh: section: 2 (over x), seq: 4 (over y, core), tp: 4 (over z).
Axes of the slice: x: 2, y: 2, z: 4, core: 2. Of those that a mesh axis runs over, the one named last changes fastest.
Arguments:
- hidden_image: bfloat16 [2, 512, 1536], P(None, 'seq'), may hold values from -6 to 6
- hidden_text: bfloat16 [2, 128, 1536], P(None, 'seq'), may hold values from -6 to 6
- latent: float32 [2, 512, 64], P(None, 'seq'), may hold values from -6 to 6
- timestep: int32 [2], replicated, may hold values from 14 to 27
- text_length: int32 [2], replicated, may hold values from 32 to 128, as said below
- text_keep: int32 [2, 128], replicated, may hold values 0 or 1
- patch_order: int32 [4], replicated, may hold values from 0 to 3, each once
- stale_image_kv: bfloat16 [2, 2, 512, 2, 1536], P('section', None, 'seq', None, 'tp'), may hold values from -160 to 160
- stale_text_kv: bfloat16 [2, 2, 128, 2, 1536], P('section', None, 'seq', None, 'tp'), may hold values from -6 to 6
- mod_image: float32 [2, 2, 6, 1536], P('section'), may hold values from -3 to 3
- mod_text: float32 [2, 2, 6, 1536], P('section'), may hold values from -3 to 3
- mod_final: float32 [2, 2, 1536], replicated, may hold values from -3 to 3
- qkv_image: bfloat16 [2, 1536, 3, 1536], P('section', None, None, 'tp'), may hold values from -0.15625 to 0.15625
- out_image: bfloat16 [2, 1536, 1536], P('section', 'tp'), may hold values from -0.15625 to 0.15625
- up_image: bfloat16 [2, 1536, 6144], P('section', None, 'tp'), may hold values from -0.15625 to 0.15625
- down_image: bfloat16 [2, 6144, 1536], P('section', 'tp'), may hold values from -0.078125 to 0.078125
- qkv_text: bfloat16 [2, 1536, 3, 1536], P('section', None, None, 'tp'), may hold values from -0.15625 to 0.15625
- out_text: bfloat16 [2, 1536, 1536], P('section', 'tp'), may hold values from -0.15625 to 0.15625
- up_text: bfloat16 [2, 1536, 6144], P('section', None, 'tp'), may hold values from -0.15625 to 0.15625
- down_text: bfloat16 [2, 6144, 1536], P('section', 'tp'), may hold values from -0.078125 to 0.078125
- final_weight: bfloat16 [1536, 64], replicated, may hold values from -0.3125 to 0.3125
Outputs:
- latent_out: float32 [2, 2, 512, 64], P('section', None, 'seq')
- image_kv_next: bfloat16 [2, 2, 512, 2, 1536], P('section', None, 'seq', None, 'tp')
- text_kv_next: bfloat16 [2, 2, 128, 2, 1536], P('section', None, 'seq', None, 'tp')
- text_hidden: bfloat16 [2, 2, 128, 1536], P('section', None, 'seq')
The draws below stay inside these ranges and needn't reach their ends.
Inputs may be any that keep to these rules, and one draw needn't show every extreme that they name: `text_length`: some request has exactly 128 text tokens.
All inputs are finite; a program needn't handle non-finite values.
Results may differ from the reference program's by a relative error of at most 0.023.
Values may be sent and summed in bfloat16 or wider, within the bound.
A program may use at most 128 MiB of HBM per device.

```python
import jax
import jax.numpy as jnp
from jax import lax

D = 1536
HEADS = 24
HD = 64
FF = 6144
CHANNELS = 64
PATCHES = 4
STEPS = 28
REQ = 2
PT = 32
TQ = 8
IMG = 512
TXT = 128
LIVE_MAX = 128
N_SEQ = 4


def draw_text_length(key, part):
    first_key, second_key = jax.random.split(jax.random.fold_in(key, 11))
    lengths = jax.random.randint(first_key, (REQ,), TXT // 4, LIVE_MAX + 1)
    chosen = jax.random.randint(second_key, (), 0, REQ)
    return jnp.where(jnp.arange(REQ) == chosen, LIVE_MAX, lengths).astype(jnp.int32)


def draw_stale_image_kv(key, part):
    shape = (2, REQ, IMG, 2, D)
    base_key = jax.random.fold_in(jax.random.fold_in(key, 23), 0)
    values = jnp.clip(jax.random.normal(base_key, shape, jnp.float32), -6.0, 6.0)
    return values.astype(jnp.bfloat16)


def place_ends(array, stream_key, low, largest):
    extent = array.shape
    index_at = [jax.random.randint(jax.random.fold_in(stream_key, axis), (), 0, extent[axis]) for axis in range(len(extent))]
    array = array.at[tuple(index_at)].set(low)
    longest = extent.index(max(extent))
    index_at[longest] = (index_at[longest] + 1) % extent[longest]
    return array.at[tuple(index_at)].set(largest)


def block_levels(stream_key, shape, cuts, least, high):
    level, own = 1.0, jax.random.fold_in(stream_key, 6)
    for axis_at, parts in cuts:
        heights = jnp.exp(jax.random.uniform(jax.random.fold_in(own, axis_at), (parts,), jnp.float32, least / len(cuts), high / len(cuts)))
        level = level * jnp.repeat(heights, shape[axis_at] // parts).reshape([-1 if axis == axis_at else 1 for axis in range(len(shape))])
    return level


def normal_values(rng, extent, scale, limit, cuts=(), held_as=jnp.bfloat16):
    entries = jax.random.normal(rng, extent, jnp.float32) * scale
    if len(cuts) > 0:
        entries = block_levels(rng, extent, cuts, -0.22, 0.18) * entries
    return jnp.clip(entries, min=-limit, max=limit).astype(held_as)


def setup_inputs(seed: int = 0) -> dict:
    key_of = jax.random.split(jax.random.key(seed), 22)
    return {
        "hidden_image": normal_values(key_of[0], (REQ, IMG, D), 1.0, 6.0, ((1, 4),)),
        "hidden_text": normal_values(key_of[1], (REQ, TXT, D), 1.0, 6.0, ((1, 4),)),
        "latent": normal_values(key_of[2], (REQ, IMG, CHANNELS), 1.0, 6.0, ((1, 4),), jnp.float32),
        "timestep": jax.random.randint(key_of[3], (REQ,), STEPS // 2, STEPS).astype(jnp.int32),
        "text_length": draw_text_length(jax.random.fold_in(key_of[21], 71), 0),
        "text_keep": place_ends((jax.random.randint(key_of[5], (REQ, TXT), 0, 2) < 1).astype(jnp.int32), jax.random.fold_in(key_of[5], 1), 0, 1),
        "patch_order": jax.random.permutation(key_of[6], PATCHES).astype(jnp.int32),
        "stale_image_kv": draw_stale_image_kv(jax.random.fold_in(key_of[21], 71), 0),
        "stale_text_kv": normal_values(key_of[8], (2, REQ, TXT, 2, D), 1.0, 6.0, ((0, 2), (2, 4), (4, 4))),
        "mod_image": normal_values(key_of[9], (2, REQ, 6, D), 0.5, 3.0, ((0, 2),), jnp.float32),
        "mod_text": normal_values(key_of[10], (2, REQ, 6, D), 0.5, 3.0, ((0, 2),), jnp.float32),
        "mod_final": normal_values(key_of[11], (REQ, 2, D), 0.5, 3.0, (), jnp.float32),
        "qkv_image": normal_values(key_of[12], (2, D, 3, D), D ** -0.5, 0.15625, ((0, 2), (3, 4))),
        "out_image": normal_values(key_of[13], (2, D, D), D ** -0.5, 0.15625, ((0, 2), (1, 4))),
        "up_image": normal_values(key_of[14], (2, D, FF), D ** -0.5, 0.15625, ((0, 2), (2, 4))),
        "down_image": normal_values(key_of[15], (2, FF, D), FF ** -0.5, 0.078125, ((0, 2), (1, 4))),
        "qkv_text": normal_values(key_of[16], (2, D, 3, D), D ** -0.5, 0.15625, ((0, 2), (3, 4))),
        "out_text": normal_values(key_of[17], (2, D, D), D ** -0.5, 0.15625, ((0, 2), (1, 4))),
        "up_text": normal_values(key_of[18], (2, D, FF), D ** -0.5, 0.15625, ((0, 2), (2, 4))),
        "down_text": normal_values(key_of[19], (2, FF, D), FF ** -0.5, 0.078125, ((0, 2), (1, 4))),
        "final_weight": normal_values(key_of[20], (D, CHANNELS), (D // 4) ** -0.5, 0.3125),
    }


EPSILON = 1e-06
NEGATIVE = -1e+30
TIME_SHIFT = 3.0

def rounded(values):
    return lax.optimization_barrier(values.astype(jnp.bfloat16)).astype(jnp.float32)

def modulate(values, shift_vec, scale_vec):
    mean_value = lax.optimization_barrier(jnp.mean(values, axis=-1, keepdims=True))
    centred = values - mean_value
    variance = lax.optimization_barrier(jnp.mean(centred * centred, axis=-1, keepdims=True))
    normed = centred * lax.rsqrt(variance + EPSILON)
    return normed * (1.0 + scale_vec[:, None, :]) + shift_vec[:, None, :]

def matmul_rows(rows, weight):
    flattened = rows.reshape(-1, rows.shape[-1])
    result = jnp.dot(flattened, weight, preferred_element_type=jnp.float32)
    return result.reshape(rows.shape[:-1] + (weight.shape[-1],))

def project(rows, modulation, weight):
    normed = modulate(rows.astype(jnp.float32), modulation[:, 0], modulation[:, 1]).astype(jnp.bfloat16)
    mixed = matmul_rows(normed, weight.reshape(weight.shape[0], -1)).astype(jnp.bfloat16)
    return mixed.reshape(rows.shape[0], rows.shape[1], 3, -1)

def finish(rows, attended, modulation, out_weight, up_weight, down_weight):
    attention = matmul_rows(attended, out_weight)
    after_attention = rows.astype(jnp.float32) + modulation[:, 2][:, None, :] * attention
    normed = modulate(after_attention, modulation[:, 3], modulation[:, 4]).astype(jnp.bfloat16)
    hidden = jax.nn.gelu(matmul_rows(normed, up_weight), approximate=True).astype(jnp.bfloat16)
    result = after_attention + modulation[:, 5][:, None, :] * matmul_rows(hidden, down_weight)
    return result.astype(jnp.bfloat16)

def attend(queries, keys_all, values_all, key_mask):
    requests = queries.shape[0]
    query_count = queries.shape[1]
    query_heads = queries.reshape(requests, query_count, HEADS, HD).astype(jnp.float32)
    key_heads = keys_all.reshape(requests, keys_all.shape[1], HEADS, HD).astype(jnp.float32)
    value_heads = values_all.reshape(requests, values_all.shape[1], HEADS, HD).astype(jnp.float32)
    scores = jnp.einsum('rqhe,rkhe->rhqk', query_heads, key_heads) * HD ** (-0.5)
    scores = jnp.where(key_mask[:, None, None, :], scores, NEGATIVE)
    rowmax = lax.optimization_barrier(jnp.max(scores, axis=-1, keepdims=True))
    exponent = jnp.where(key_mask[:, None, None, :], jnp.exp(scores - rowmax), 0.0)
    totals = lax.optimization_barrier(jnp.sum(exponent, axis=-1))
    summed = jnp.einsum('rhqk,rkhe->rhqe', rounded(exponent), value_heads)
    result = summed / totals[..., None]
    return jnp.transpose(result, (0, 2, 1, 3)).reshape(requests, query_count, HEADS * HD).astype(jnp.bfloat16)

def sigma_of(index_value):
    progress = 1.0 - index_value / STEPS
    return TIME_SHIFT * progress / (1.0 + (TIME_SHIFT - 1.0) * progress)

def reference(hidden_image, hidden_text, latent, timestep, text_length, text_keep, patch_order, stale_image_kv, stale_text_kv, mod_image, mod_text, mod_final, qkv_image, out_image, up_image, down_image, qkv_text, out_text, up_text, down_text, final_weight):
    positions = jnp.arange(TXT, dtype=jnp.int32)
    valid_text = (positions[None, :] < text_length[:, None]) & (text_keep == 1)
    valid_all = jnp.concatenate([jnp.ones((REQ, IMG), jnp.bool_), valid_text], axis=1)
    image_rows = hidden_image.reshape(REQ, N_SEQ, PATCHES, PT, D)
    text_rows = hidden_text.reshape(REQ, N_SEQ, PATCHES, TQ, D)
    image_kv_list = []
    text_kv_list = []
    text_hidden_list = []
    for layer_index in range(2):
        image_buffer = stale_image_kv[layer_index].reshape(REQ, N_SEQ, PATCHES, PT, 2, D)
        text_buffer = stale_text_kv[layer_index].reshape(REQ, N_SEQ, PATCHES, TQ, 2, D)
        image_result = jnp.zeros_like(image_rows)
        text_result = jnp.zeros_like(text_rows)
        for slot_index in range(PATCHES):
            patch_index = patch_order[slot_index]
            own_image = lax.dynamic_index_in_dim(image_rows, patch_index, 2, keepdims=False).reshape(REQ, N_SEQ * PT, D)
            own_text = text_rows[:, :, slot_index].reshape(REQ, N_SEQ * TQ, D)
            image_qkv = project(own_image, mod_image[layer_index], qkv_image[layer_index])
            text_qkv = project(own_text, mod_text[layer_index], qkv_text[layer_index])
            image_buffer = lax.dynamic_update_index_in_dim(image_buffer, image_qkv[:, :, 1:].reshape(REQ, N_SEQ, PT, 2, D), patch_index, 2)
            text_buffer = text_buffer.at[:, :, slot_index].set(text_qkv[:, :, 1:].reshape(REQ, N_SEQ, TQ, 2, D))
            keys_all = jnp.concatenate([image_buffer.reshape(REQ, IMG, 2, D), text_buffer.reshape(REQ, TXT, 2, D)], axis=1)
            queries = jnp.concatenate([image_qkv[:, :, 0], text_qkv[:, :, 0]], axis=1)
            attended = attend(queries, keys_all[:, :, 0], keys_all[:, :, 1], valid_all)
            image_new = finish(own_image, attended[:, :N_SEQ * PT], mod_image[layer_index], out_image[layer_index], up_image[layer_index], down_image[layer_index])
            text_new = finish(own_text, attended[:, N_SEQ * PT:], mod_text[layer_index], out_text[layer_index], up_text[layer_index], down_text[layer_index])
            image_result = lax.dynamic_update_index_in_dim(image_result, image_new.reshape(REQ, N_SEQ, PT, D), patch_index, 2)
            text_result = text_result.at[:, :, slot_index].set(text_new.reshape(REQ, N_SEQ, TQ, D))
        image_kv_list.append(image_buffer.reshape(REQ, IMG, 2, D))
        text_kv_list.append(text_buffer.reshape(REQ, TXT, 2, D))
        text_hidden_list.append(text_result.reshape(REQ, TXT, D))
        image_rows = image_result
        text_rows = text_result
    final_rows = modulate(image_rows.reshape(REQ, IMG, D).astype(jnp.float32), mod_final[:, 0], mod_final[:, 1]).astype(jnp.bfloat16)
    velocity = matmul_rows(final_rows, final_weight)
    index_value = timestep.astype(jnp.float32)
    sigma_now = sigma_of(index_value)
    sigma_next = sigma_of(index_value + 1.0)
    next_latent = latent + (sigma_next - sigma_now)[:, None, None] * velocity
    denoised = latent - sigma_now[:, None, None] * velocity
    return (jnp.stack([next_latent, denoised]), jnp.stack(image_kv_list), jnp.stack(text_kv_list), jnp.stack(text_hidden_list))
```

```python
import jax
import jax.numpy as jnp
from jax import lax
from jax.sharding import PartitionSpec as P

HD = 64
STEPS = 28


EPSILON = 1e-06
NEGATIVE = -1e30
TIME_SHIFT = 3.0


def row_norm(values, shift_rows, scale_rows):
    mean_value = jnp.mean(values, axis=-1, keepdims=True)
    centred = values - mean_value
    variance = jnp.mean(centred * centred, axis=-1, keepdims=True)
    return centred * lax.rsqrt(variance + EPSILON) * (1.0 + scale_rows) + shift_rows


def sigma_of(index_value):
    progress = 1.0 - index_value / STEPS
    return TIME_SHIFT * progress / (1.0 + (TIME_SHIFT - 1.0) * progress)


def attend(queries, keys, values, allowed):
    heads = queries.shape[1] // HD
    split = lambda rows: rows.reshape(rows.shape[0], heads, HD)
    scores = jnp.einsum(
        "qhe,khe->hqk", split(queries), split(keys), preferred_element_type=jnp.float32
    ) * HD ** (-0.5)
    scores = jnp.where(allowed[None], scores, NEGATIVE)
    rowmax = jnp.max(scores, axis=-1, keepdims=True)
    exponent = jnp.where(allowed[None], jnp.exp(scores - rowmax), 0.0)
    totals = jnp.sum(exponent, axis=-1)
    summed = jnp.einsum(
        "hqk,khe->hqe",
        exponent.astype(jnp.bfloat16),
        split(values),
        preferred_element_type=jnp.float32,
    )
    result = summed / totals[..., None]
    return jnp.transpose(result, (1, 0, 2)).reshape(queries.shape).astype(jnp.bfloat16)


def allowed_keys(patch_order, live, image_local, text_local, seq_count):
    slot_count = patch_order.shape[0]
    order = jnp.arange(slot_count, dtype=jnp.int32)
    rank = jnp.sum(
        jnp.where(patch_order[:, None] == order[None, :], order[:, None], 0), axis=0
    )
    local = jnp.concatenate(
        [
            jnp.repeat(rank, image_local // slot_count),
            jnp.repeat(order, text_local // slot_count),
        ]
    )
    keys = jnp.tile(local, seq_count)
    fresh = keys[None, :] <= local[:, None]
    kept = jnp.concatenate(
        [
            jnp.ones((live.shape[0], seq_count, image_local), jnp.bool_),
            live.reshape(live.shape[0], seq_count, text_local),
        ],
        axis=2,
    ).reshape(live.shape[0], 1, -1)
    return jnp.concatenate([fresh[None] & kept, ~fresh[None] & kept], axis=2)


def on_device(
    hidden_image,
    hidden_text,
    latent,
    timestep,
    text_length,
    text_keep,
    patch_order,
    stale_image_kv,
    stale_text_kv,
    mod_image,
    mod_text,
    mod_final,
    qkv_image,
    out_image,
    up_image,
    down_image,
    qkv_text,
    out_text,
    up_text,
    down_text,
    final_weight,
):
    requests, image_local, model_width = hidden_image.shape
    text_local = hidden_text.shape[1]
    local_width = qkv_image.shape[3]
    seq_count = lax.axis_size("seq")
    section_index = lax.axis_index("section")
    first_section = section_index == 0
    text_total = text_keep.shape[1]
    positions = jnp.arange(text_total, dtype=jnp.int32)
    live = (positions[None, :] < text_length[:, None]) & (text_keep == 1)
    allowed = allowed_keys(patch_order, live, image_local, text_local, seq_count)
    stale_local = jnp.concatenate(
        [
            stale_image_kv[0].reshape(requests, image_local, 2 * local_width),
            stale_text_kv[0].reshape(requests, text_local, 2 * local_width),
        ],
        axis=1,
    )
    stale = lax.all_gather(stale_local, "seq", axis=1, tiled=True)
    qkv_i = qkv_image[0].reshape(model_width, -1)
    qkv_t = qkv_text[0].reshape(model_width, -1)
    inputs = jnp.concatenate([hidden_image, hidden_text], axis=1)
    arrived = None
    made_rows, made_kv = [], []
    for moment in range(requests + 1):
        request = jnp.clip(moment - section_index, 0, requests - 1)
        pick = lambda values: lax.dynamic_index_in_dim(values, request, 0, keepdims=False)
        rows = inputs[0] if moment == 0 else jnp.where(first_section, pick(inputs), arrived)
        mi, mt = pick(mod_image[0]), pick(mod_text[0])
        image_rows = rows[:image_local].astype(jnp.float32)
        text_rows = rows[image_local:].astype(jnp.float32)
        norm_i = row_norm(image_rows, mi[0], mi[1]).astype(jnp.bfloat16)
        norm_t = row_norm(text_rows, mt[0], mt[1]).astype(jnp.bfloat16)
        dot = lambda left, right: jnp.dot(left, right, preferred_element_type=jnp.float32)
        mixed = jnp.concatenate([dot(norm_i, qkv_i), dot(norm_t, qkv_t)], axis=0).astype(
            jnp.bfloat16
        )
        queries, fresh_local = mixed[:, :local_width], mixed[:, local_width:]
        fresh = lax.all_gather(fresh_local, "seq", axis=0, tiled=True)
        both = jnp.concatenate([fresh, pick(stale)], axis=0)
        attended = attend(
            queries, both[:, :local_width], both[:, local_width:], pick(allowed)
        )
        part = jnp.concatenate(
            [dot(attended[:image_local], out_image[0]), dot(attended[image_local:], out_text[0])],
            axis=0,
        )
        summed = lax.psum(part.astype(jnp.bfloat16), "tp").astype(jnp.float32)
        image_first = image_rows + mi[2] * summed[:image_local]
        text_first = text_rows + mt[2] * summed[image_local:]
        norm_i = row_norm(image_first, mi[3], mi[4]).astype(jnp.bfloat16)
        norm_t = row_norm(text_first, mt[3], mt[4]).astype(jnp.bfloat16)
        act = lambda values: jax.nn.gelu(values, approximate=True).astype(jnp.bfloat16)
        part = jnp.concatenate(
            [
                dot(act(dot(norm_i, up_image[0])), down_image[0]),
                dot(act(dot(norm_t, up_text[0])), down_text[0]),
            ],
            axis=0,
        )
        summed = lax.psum(part.astype(jnp.bfloat16), "tp").astype(jnp.float32)
        new_rows = jnp.concatenate(
            [image_first + mi[5] * summed[:image_local], text_first + mt[5] * summed[image_local:]],
            axis=0,
        ).astype(jnp.bfloat16)
        made_rows.append(new_rows)
        made_kv.append(fresh_local)
        if moment < requests:
            arrived = lax.ppermute(new_rows, "section", [(0, 1)])
    choose = lambda made: jnp.stack(
        [jnp.where(first_section, made[r], made[r + 1]) for r in range(requests)]
    )
    rows_out, kv_out = choose(made_rows), choose(made_kv)
    final_normed = row_norm(
        rows_out[:, :image_local].astype(jnp.float32), mod_final[:, :1], mod_final[:, 1:]
    ).astype(jnp.bfloat16)
    velocity = jnp.dot(
        final_normed.reshape(-1, model_width), final_weight, preferred_element_type=jnp.float32
    ).reshape(requests, image_local, -1)
    returned = lax.ppermute(velocity.astype(jnp.bfloat16), "section", [(1, 0)])
    velocity_used = jnp.where(first_section, returned.astype(velocity.dtype), velocity)
    index_value = timestep.astype(jnp.float32)
    sigma_now = sigma_of(index_value)
    sigma_next = sigma_of(index_value + 1.0)
    stepped = latent + (sigma_next - sigma_now)[:, None, None] * velocity_used
    denoised = latent - sigma_now[:, None, None] * velocity_used
    latent_part = jnp.where(first_section, stepped, denoised)[None]
    return (
        latent_part,
        kv_out[:, :image_local].reshape(requests, image_local, 2, local_width)[None],
        kv_out[:, image_local:].reshape(requests, text_local, 2, local_width)[None],
        rows_out[:, image_local:][None],
    )


def solution(mesh):
    in_specs = (
        P(None, "seq", None),
        P(None, "seq", None),
        P(None, "seq", None),
        P(),
        P(),
        P(),
        P(),
        P("section", None, "seq", None, "tp"),
        P("section", None, "seq", None, "tp"),
        P("section", None, None, None),
        P("section", None, None, None),
        P(),
        P("section", None, None, "tp"),
        P("section", "tp", None),
        P("section", None, "tp"),
        P("section", "tp", None),
        P("section", None, None, "tp"),
        P("section", "tp", None),
        P("section", None, "tp"),
        P("section", "tp", None),
        P(),
    )
    out_specs = (
        P("section", None, "seq", None),
        P("section", None, "seq", None, "tp"),
        P("section", None, "seq", None, "tp"),
        P("section", None, "seq", None),
    )
    return jax.shard_map(
        on_device, mesh=mesh, in_specs=in_specs, out_specs=out_specs, check_vma=False
    )
```

```python
import functools

import jax
import jax.numpy as jnp
from jax import lax
from jax.experimental import pallas as pl
from jax.experimental.pallas import tpu as pltpu
from jax.sharding import PartitionSpec as P

HD = 64
STEPS = 28


EPSILON = 1e-06
NEGATIVE = -1e30
TIME_SHIFT = 3.0


def row_norm(values, shift_rows, scale_rows):
    mean_value = jnp.mean(values, axis=-1, keepdims=True)
    centred = values - mean_value
    variance = jnp.mean(centred * centred, axis=-1, keepdims=True)
    return centred * lax.rsqrt(variance + EPSILON) * (1.0 + scale_rows) + shift_rows


def pack(values):
    half = values.shape[1] // 2
    return jnp.concatenate([values[:, :half], values[:, half:]], axis=0).astype(jnp.bfloat16)


def unpack(block):
    wide = block.astype(jnp.float32)
    rows = wide.shape[0] // 2
    return jnp.concatenate([wide[:rows], wide[rows:]], axis=1)


def finish_kernel(n, image_rows, text_rows, last, *refs):
    refs = list(refs)
    take = lambda count: [refs.pop(0) for _ in range(count)]
    attended, shard, mod = take(3)
    if not last:
        following, mod_following = take(2)
    weights = take(6)
    if last:
        (new_shard,) = take(1)
    else:
        new_shard, next_normed, next_shard = take(3)
    held = take(6)
    part, first, send, arrive, gather, normed_i, normed_t, hidden_i, hidden_t, weight_sems = take(10)
    send_sems, recv_sems, gather_send_sems, gather_recv_sems = take(4)
    if not last:
        passed, passed_to, pass_sems, next_gather = take(4)
    me = lax.axis_index("tp")
    section = lax.axis_index("section")
    loads = [
        pltpu.make_async_copy(weights[i], held[i], weight_sems.at[i]) for i in range(6)
    ]
    for load in loads:
        load.start()
    peers = [lax.rem(me + d, n) for d in range(1, n)]
    barrier = pltpu.get_barrier_semaphore()
    for peer in peers:
        pl.semaphore_signal(
            barrier, inc=1, device_id={"tp": peer}, device_id_type=pl.DeviceIdType.MESH
        )
    if not last:
        pl.semaphore_signal(
            barrier,
            inc=1,
            device_id={"section": 1 - section},
            device_id_type=pl.DeviceIdType.MESH,
        )
    out_i, out_t, up_i, up_t, down_i, down_t = held
    width = shard.shape[1]
    step = min(512, width)
    all_images = image_rows * n

    def product(left_i, left_t, right_i, right_t):
        @pl.loop(0, width // step)
        def _(index):
            columns = pl.ds(pl.multiple_of(index * step, step), step)
            part[:all_images, columns] = jnp.dot(
                left_i, right_i[:, columns], preferred_element_type=jnp.float32
            )
            part[all_images:, columns] = jnp.dot(
                left_t, right_t[:, columns], preferred_element_type=jnp.float32
            )

    def scatter_sum(phase):
        for j in range(n):
            send[phase, j] = pack(
                jnp.concatenate(
                    [
                        part[j * image_rows : (j + 1) * image_rows],
                        part[all_images + j * text_rows : all_images + (j + 1) * text_rows],
                    ],
                    axis=0,
                )
            )
        copies = []
        for d in range(1, n):
            copies.append(
                pltpu.make_async_remote_copy(
                    src_ref=send.at[phase, peers[d - 1]],
                    dst_ref=arrive.at[phase, d - 1],
                    send_sem=send_sems.at[phase, d - 1],
                    recv_sem=recv_sems.at[phase, d - 1],
                    device_id={"tp": peers[d - 1]},
                    device_id_type=pl.DeviceIdType.MESH,
                )
            )
            copies[-1].start()
        total = unpack(send[phase, me])
        for d in range(1, n):
            copies[d - 1].wait_recv()
            total = total + unpack(arrive[phase, d - 1])
        return total, copies

    def gather_rows(phase, buffer):
        copies = []
        for d in range(1, n):
            copies.append(
                pltpu.make_async_remote_copy(
                    src_ref=buffer.at[me],
                    dst_ref=buffer.at[me],
                    send_sem=gather_send_sems.at[phase, d - 1],
                    recv_sem=gather_recv_sems.at[phase, d - 1],
                    device_id={"tp": peers[d - 1]},
                    device_id_type=pl.DeviceIdType.MESH,
                )
            )
            copies[-1].start()
        for copy in copies:
            copy.wait_recv()
        return copies

    def both(values, table, function):
        return jnp.concatenate(
            [
                function(values[:image_rows], table[0]),
                function(values[image_rows:], table[1]),
            ],
            axis=0,
        )

    loads[0].wait()
    loads[1].wait()
    product(attended[:all_images], attended[all_images:], out_i, out_t)
    pl.semaphore_wait(barrier, n - 1 if last else n)
    total, pending = scatter_sum(0)
    first[...] = shard[...] + both(total, mod, lambda rows, table: table[2:3] * rows)
    gather[me] = pack(
        both(first[...], mod, lambda rows, table: row_norm(rows, table[3:4], table[4:5]))
    )
    pending += gather_rows(0, gather)
    text_parts = []
    for j in range(n):
        block = unpack(gather[j])
        normed_i[j * image_rows : (j + 1) * image_rows] = block[:image_rows].astype(jnp.bfloat16)
        text_parts.append(block[image_rows:])
    normed_t[...] = jnp.concatenate(text_parts, axis=0).astype(jnp.bfloat16)
    loads[2].wait()
    loads[3].wait()

    @pl.loop(0, up_i.shape[1] // step)
    def _(index):
        columns = pl.ds(pl.multiple_of(index * step, step), step)
        for normed, up, hidden in ((normed_i, up_i, hidden_i), (normed_t, up_t, hidden_t)):
            hidden[:, columns] = jax.nn.gelu(
                jnp.dot(normed[...], up[:, columns], preferred_element_type=jnp.float32),
                approximate=True,
            ).astype(jnp.bfloat16)

    loads[4].wait()
    loads[5].wait()
    product(hidden_i[...], hidden_t[...], down_i, down_t)
    total, more = scatter_sum(1)
    pending += more
    made = (first[...] + both(total, mod, lambda rows, table: table[5:6] * rows)).astype(
        jnp.bfloat16
    )
    new_shard[...] = made
    if not last:
        passed[...] = pack(made.astype(jnp.float32))
        copy = pltpu.make_async_remote_copy(
            src_ref=passed,
            dst_ref=passed_to,
            send_sem=pass_sems.at[0],
            recv_sem=pass_sems.at[1],
            device_id={"section": 1 - section},
            device_id_type=pl.DeviceIdType.MESH,
        )
        copy.start()
        copy.wait_recv()
        pending.append(copy)
        next_shard[...] = jnp.where(section == 0, following[...], unpack(passed_to[...]))
        next_gather[me] = pack(
            both(
                next_shard[...],
                mod_following,
                lambda rows, table: row_norm(rows, table[0:1], table[1:2]),
            )
        )
        pending += gather_rows(1, next_gather)
        text_parts = []
        for j in range(n):
            block = unpack(next_gather[j])
            next_normed[j * image_rows : (j + 1) * image_rows] = block[:image_rows].astype(
                jnp.bfloat16
            )
            text_parts.append(block[image_rows:])
        next_normed[all_images:] = jnp.concatenate(text_parts, axis=0).astype(jnp.bfloat16)
    for copy in pending:
        copy.wait_send()


def finish(n, attended, shard, mod, following, mod_following, weights):
    last = following is None
    rows, width = attended.shape[0], shard.shape[1]
    shard_rows = shard.shape[0]
    image_rows = shard_rows * 4 // 5
    hidden_width = weights[2].shape[1]
    vmem = pl.BlockSpec(memory_space=pltpu.VMEM)
    anywhere = pl.BlockSpec(memory_space=pl.ANY)
    block = (2 * shard_rows, width // 2)
    bf16, f32 = jnp.bfloat16, jnp.float32
    operands = [attended, shard, mod] + ([] if last else [following, mod_following])
    out_shape = [jax.ShapeDtypeStruct((shard_rows, width), bf16)]
    if not last:
        out_shape += [
            jax.ShapeDtypeStruct((rows, width), bf16),
            jax.ShapeDtypeStruct((shard_rows, width), f32),
        ]
    images = image_rows * n
    texts = rows - images
    scratch = [pltpu.VMEM(weight.shape, bf16) for weight in weights]
    scratch += [
        pltpu.VMEM((rows, width), f32),
        pltpu.VMEM((shard_rows, width), f32),
        pltpu.VMEM((2, n) + block, bf16),
        pltpu.VMEM((2, n - 1) + block, bf16),
        pltpu.VMEM((n,) + block, bf16),
        pltpu.VMEM((images, width), bf16),
        pltpu.VMEM((texts, width), bf16),
        pltpu.VMEM((images, hidden_width), bf16),
        pltpu.VMEM((texts, hidden_width), bf16),
        pltpu.SemaphoreType.DMA((6,)),
    ]
    scratch += [pltpu.SemaphoreType.DMA((2, n - 1))] * 4
    if not last:
        scratch += [
            pltpu.VMEM(block, bf16),
            pltpu.VMEM(block, bf16),
            pltpu.SemaphoreType.DMA((2,)),
            pltpu.VMEM((n,) + block, bf16),
        ]
    return pl.pallas_call(
        functools.partial(finish_kernel, n, image_rows, shard_rows - image_rows, last),
        out_shape=out_shape,
        in_specs=[vmem] * len(operands) + [anywhere] * 6,
        out_specs=[vmem] * len(out_shape),
        scratch_shapes=scratch,
        compiler_params=pltpu.CompilerParams(
            collective_id=1 if last else 0,
            has_side_effects=True,
            vmem_limit_bytes=48 * 1024 * 1024,
        ),
    )(*operands, *weights)


def sigma_of(index_value):
    progress = 1.0 - index_value / STEPS
    return TIME_SHIFT * progress / (1.0 + (TIME_SHIFT - 1.0) * progress)


def attend(queries, keys, values, allowed):
    heads = queries.shape[1] // HD
    split = lambda rows: rows.reshape(rows.shape[0], heads, HD)
    scores = jnp.einsum(
        "qhe,khe->hqk", split(queries), split(keys), preferred_element_type=jnp.float32
    ) * HD ** (-0.5)
    scores = jnp.where(allowed[None], scores, NEGATIVE)
    rowmax = jnp.max(scores, axis=-1, keepdims=True)
    exponent = jnp.where(allowed[None], jnp.exp(scores - rowmax), 0.0)
    totals = jnp.sum(exponent, axis=-1)
    summed = jnp.einsum(
        "hqk,khe->hqe",
        exponent.astype(jnp.bfloat16),
        split(values),
        preferred_element_type=jnp.float32,
    )
    result = summed / totals[..., None]
    return jnp.transpose(result, (1, 0, 2)).reshape(queries.shape).astype(jnp.bfloat16)


def allowed_keys(patch_order, live, image_local, text_local, seq_count):
    slot_count = patch_order.shape[0]
    order = jnp.arange(slot_count, dtype=jnp.int32)
    rank = jnp.sum(
        jnp.where(patch_order[:, None] == order[None, :], order[:, None], 0), axis=0
    )
    local = jnp.concatenate(
        [
            jnp.repeat(rank, image_local // slot_count),
            jnp.repeat(order, text_local // slot_count),
        ]
    )
    keys = jnp.tile(local, seq_count)
    fresh = keys[None, :] <= local[:, None]
    kept = jnp.concatenate(
        [
            jnp.ones((live.shape[0], seq_count, image_local), jnp.bool_),
            live.reshape(live.shape[0], seq_count, text_local),
        ],
        axis=2,
    ).reshape(live.shape[0], 1, -1)
    return jnp.concatenate([fresh[None] & kept, ~fresh[None] & kept], axis=2)


def on_device(
    hidden_image,
    hidden_text,
    latent,
    timestep,
    text_length,
    text_keep,
    patch_order,
    stale_image_kv,
    stale_text_kv,
    mod_image,
    mod_text,
    mod_final,
    qkv_image,
    out_image,
    up_image,
    down_image,
    qkv_text,
    out_text,
    up_text,
    down_text,
    final_weight,
):
    requests, image_local, model_width = hidden_image.shape
    text_local = hidden_text.shape[1]
    local_width = qkv_image.shape[3]
    seq_count = lax.axis_size("seq")
    section_index = lax.axis_index("section")
    first_section = section_index == 0
    text_total = text_keep.shape[1]
    positions = jnp.arange(text_total, dtype=jnp.int32)
    live = (positions[None, :] < text_length[:, None]) & (text_keep == 1)
    allowed = allowed_keys(patch_order, live, image_local, text_local, seq_count)
    stale_local = jnp.concatenate(
        [
            stale_image_kv[0].reshape(requests, image_local, 2 * local_width),
            stale_text_kv[0].reshape(requests, text_local, 2 * local_width),
        ],
        axis=1,
    )
    stale = lax.all_gather(stale_local, "seq", axis=1, tiled=True)
    tp_size = lax.axis_size("tp")
    shapes_fit = (
        image_local == 4 * text_local
        and text_local % (8 * tp_size) == 0
        and local_width % 128 == 0
    )
    if shapes_fit:
        tp_count = lax.axis_size("tp")
        qkv_i = qkv_image[0].reshape(model_width, -1)
        qkv_t = qkv_text[0].reshape(model_width, -1)
        tp_index = lax.axis_index("tp")
        image_shard, text_shard = image_local // tp_count, text_local // tp_count
        shards = jnp.concatenate(
            [
                lax.dynamic_slice_in_dim(hidden_image, tp_index * image_shard, image_shard, 1),
                lax.dynamic_slice_in_dim(hidden_text, tp_index * text_shard, text_shard, 1),
            ],
            axis=1,
        ).astype(jnp.float32)
        mods = jnp.stack([mod_image[0], mod_text[0]], axis=1)
        weights = [
            value[0] for value in (out_image, out_text, up_image, up_text, down_image, down_text)
        ]
        dot = lambda left, right: jnp.dot(left, right, preferred_element_type=jnp.float32)

        def picker(moment):
            request = jnp.clip(moment - section_index, 0, requests - 1)
            return lambda values: lax.dynamic_index_in_dim(values, request, 0, keepdims=False)

        shard = shards[0]
        mod = mods[0]
        normed = jnp.concatenate(
            [
                row_norm(hidden_image[0].astype(jnp.float32), mod[0, 0], mod[0, 1]),
                row_norm(hidden_text[0].astype(jnp.float32), mod[1, 0], mod[1, 1]),
            ],
            axis=0,
        ).astype(jnp.bfloat16)
        made_rows, made_kv = [], []
        for moment in range(requests + 1):
            pick = picker(moment)
            mixed = jnp.concatenate(
                [dot(normed[:image_local], qkv_i), dot(normed[image_local:], qkv_t)], axis=0
            ).astype(jnp.bfloat16)
            queries, fresh_local = mixed[:, :local_width], mixed[:, local_width:]
            fresh = lax.all_gather(fresh_local, "seq", axis=0, tiled=True)
            both = jnp.concatenate([fresh, pick(stale)], axis=0)
            attended = attend(queries, both[:, :local_width], both[:, local_width:], pick(allowed))
            made_kv.append(fresh_local)
            if moment < requests:
                following = picker(moment + 1)
                new_rows, normed, next_shard = finish(
                    tp_count, attended, shard, mod, following(shards), following(mods), weights
                )
                shard, mod = next_shard, following(mods)
            else:
                (new_rows,) = finish(tp_count, attended, shard, mod, None, None, weights)
            made_rows.append(new_rows)
        choose = lambda made: jnp.stack(
            [jnp.where(first_section, made[r], made[r + 1]) for r in range(requests)]
        )
        shard_out, kv_out = choose(made_rows), choose(made_kv)
        text_out = lax.all_gather(shard_out[:, image_shard:], "tp", axis=1, tiled=True)
        final_normed = row_norm(
            shard_out[:, :image_shard].astype(jnp.float32), mod_final[:, :1], mod_final[:, 1:]
        ).astype(jnp.bfloat16)
        velocity = dot(final_normed.reshape(-1, model_width), final_weight).reshape(
            requests, image_shard, -1
        )
        gathered = lax.all_gather(velocity, ("section", "tp"), axis=0)
        velocity_used = jnp.concatenate(list(gathered[tp_count:]), axis=1)
    else:
        qkv_i = qkv_image[0].reshape(model_width, -1)
        qkv_t = qkv_text[0].reshape(model_width, -1)
        inputs = jnp.concatenate([hidden_image, hidden_text], axis=1)
        arrived = None
        made_rows, made_kv = [], []
        for moment in range(requests + 1):
            request = jnp.clip(moment - section_index, 0, requests - 1)
            pick = lambda values: lax.dynamic_index_in_dim(values, request, 0, keepdims=False)
            rows = inputs[0] if moment == 0 else jnp.where(first_section, pick(inputs), arrived)
            mi, mt = pick(mod_image[0]), pick(mod_text[0])
            image_rows = rows[:image_local].astype(jnp.float32)
            text_rows = rows[image_local:].astype(jnp.float32)
            norm_i = row_norm(image_rows, mi[0], mi[1]).astype(jnp.bfloat16)
            norm_t = row_norm(text_rows, mt[0], mt[1]).astype(jnp.bfloat16)
            dot = lambda left, right: jnp.dot(left, right, preferred_element_type=jnp.float32)
            mixed = jnp.concatenate([dot(norm_i, qkv_i), dot(norm_t, qkv_t)], axis=0).astype(
                jnp.bfloat16
            )
            queries, fresh_local = mixed[:, :local_width], mixed[:, local_width:]
            fresh = lax.all_gather(fresh_local, "seq", axis=0, tiled=True)
            both = jnp.concatenate([fresh, pick(stale)], axis=0)
            attended = attend(
                queries, both[:, :local_width], both[:, local_width:], pick(allowed)
            )
            part = jnp.concatenate(
                [dot(attended[:image_local], out_image[0]), dot(attended[image_local:], out_text[0])],
                axis=0,
            )
            summed = lax.psum(part.astype(jnp.bfloat16), "tp").astype(jnp.float32)
            image_first = image_rows + mi[2] * summed[:image_local]
            text_first = text_rows + mt[2] * summed[image_local:]
            norm_i = row_norm(image_first, mi[3], mi[4]).astype(jnp.bfloat16)
            norm_t = row_norm(text_first, mt[3], mt[4]).astype(jnp.bfloat16)
            act = lambda values: jax.nn.gelu(values, approximate=True).astype(jnp.bfloat16)
            part = jnp.concatenate(
                [
                    dot(act(dot(norm_i, up_image[0])), down_image[0]),
                    dot(act(dot(norm_t, up_text[0])), down_text[0]),
                ],
                axis=0,
            )
            summed = lax.psum(part.astype(jnp.bfloat16), "tp").astype(jnp.float32)
            new_rows = jnp.concatenate(
                [image_first + mi[5] * summed[:image_local], text_first + mt[5] * summed[image_local:]],
                axis=0,
            ).astype(jnp.bfloat16)
            made_rows.append(new_rows)
            made_kv.append(fresh_local)
            if moment < requests:
                arrived = lax.ppermute(new_rows, "section", [(0, 1)])
        choose = lambda made: jnp.stack(
            [jnp.where(first_section, made[r], made[r + 1]) for r in range(requests)]
        )
        rows_out, kv_out = choose(made_rows), choose(made_kv)
        final_normed = row_norm(
            rows_out[:, :image_local].astype(jnp.float32), mod_final[:, :1], mod_final[:, 1:]
        ).astype(jnp.bfloat16)
        velocity = jnp.dot(
            final_normed.reshape(-1, model_width), final_weight, preferred_element_type=jnp.float32
        ).reshape(requests, image_local, -1)
        returned = lax.ppermute(velocity.astype(jnp.bfloat16), "section", [(1, 0)])
        velocity_used = jnp.where(first_section, returned.astype(velocity.dtype), velocity)
        text_out = rows_out[:, image_local:]
    index_value = timestep.astype(jnp.float32)
    sigma_now = sigma_of(index_value)
    sigma_next = sigma_of(index_value + 1.0)
    stepped = latent + (sigma_next - sigma_now)[:, None, None] * velocity_used
    denoised = latent - sigma_now[:, None, None] * velocity_used
    latent_part = jnp.where(first_section, stepped, denoised)[None]
    return (
        latent_part,
        kv_out[:, :image_local].reshape(requests, image_local, 2, local_width)[None],
        kv_out[:, image_local:].reshape(requests, text_local, 2, local_width)[None],
        text_out[None],
    )


def solution(mesh):
    in_specs = (
        P(None, "seq", None),
        P(None, "seq", None),
        P(None, "seq", None),
        P(),
        P(),
        P(),
        P(),
        P("section", None, "seq", None, "tp"),
        P("section", None, "seq", None, "tp"),
        P("section", None, None, None),
        P("section", None, None, None),
        P(),
        P("section", None, None, "tp"),
        P("section", "tp", None),
        P("section", None, "tp"),
        P("section", "tp", None),
        P("section", None, None, "tp"),
        P("section", "tp", None),
        P("section", None, "tp"),
        P("section", "tp", None),
        P(),
    )
    out_specs = (
        P("section", None, "seq", None),
        P("section", None, "seq", None, "tp"),
        P("section", None, "seq", None, "tp"),
        P("section", None, "seq", None),
    )
    return jax.shard_map(
        on_device, mesh=mesh, in_specs=in_specs, out_specs=out_specs, check_vma=False
    )
```

```python
import functools

import jax
import jax.numpy as jnp
from jax import lax
from jax.experimental import pallas as pl
from jax.experimental.pallas import tpu as pltpu
from jax.sharding import PartitionSpec as P

HD = 64
STEPS = 28


EPSILON = 1e-06
NEGATIVE = -1e30
TIME_SHIFT = 3.0


def row_norm(values, shift_rows, scale_rows):
    mean_value = jnp.mean(values, axis=-1, keepdims=True)
    centred = values - mean_value
    variance = jnp.mean(centred * centred, axis=-1, keepdims=True)
    return centred * lax.rsqrt(variance + EPSILON) * (1.0 + scale_rows) + shift_rows


def pack(values):
    half = values.shape[1] // 2
    return jnp.concatenate([values[:, :half], values[:, half:]], axis=0).astype(jnp.bfloat16)


def unpack(block):
    wide = block.astype(jnp.float32)
    rows = wide.shape[0] // 2
    return jnp.concatenate([wide[:rows], wide[rows:]], axis=1)


def finish_kernel(n, image_rows, text_rows, last, *refs):
    refs = list(refs)
    take = lambda count: [refs.pop(0) for _ in range(count)]
    attended, shard, mod = take(3)
    if last:
        earlier, other, mod_last, final = take(4)
    else:
        following, mod_following = take(2)
    weights = take(6)
    if last:
        text_all, velocity_all = take(2)
    else:
        new_shard, next_normed, next_shard = take(3)
    held = take(6)
    part, first, send, arrive, gather, normed_i, normed_t, hidden_i, hidden_t, weight_sems = take(10)
    send_sems, recv_sems, gather_send_sems, gather_recv_sems = take(4)
    passed, passed_to, pass_sems, next_gather = take(4)
    if last:
        velocity_gather, velocity_send_sems, velocity_recv_sems = take(3)
    me = lax.axis_index("tp")
    section = lax.axis_index("section")
    loads = [
        pltpu.make_async_copy(weights[i], held[i], weight_sems.at[i]) for i in range(6)
    ]
    for load in loads:
        load.start()
    peers = [lax.rem(me + d, n) for d in range(1, n)]
    barrier = pltpu.get_barrier_semaphore()
    for peer in peers:
        pl.semaphore_signal(
            barrier, inc=1, device_id={"tp": peer}, device_id_type=pl.DeviceIdType.MESH
        )
    pl.semaphore_signal(
        barrier,
        inc=1,
        device_id={"section": 1 - section},
        device_id_type=pl.DeviceIdType.MESH,
    )
    out_i, out_t, up_i, up_t, down_i, down_t = held
    width = shard.shape[1]
    step = min(512, width)
    all_images = image_rows * n

    def product(left_i, left_t, right_i, right_t):
        @pl.loop(0, width // step)
        def _(index):
            columns = pl.ds(pl.multiple_of(index * step, step), step)
            part[:all_images, columns] = jnp.dot(
                left_i, right_i[:, columns], preferred_element_type=jnp.float32
            )
            part[all_images:, columns] = jnp.dot(
                left_t, right_t[:, columns], preferred_element_type=jnp.float32
            )

    def scatter_sum(phase):
        for j in range(n):
            send[phase, j] = pack(
                jnp.concatenate(
                    [
                        part[j * image_rows : (j + 1) * image_rows],
                        part[all_images + j * text_rows : all_images + (j + 1) * text_rows],
                    ],
                    axis=0,
                )
            )
        copies = []
        for d in range(1, n):
            copies.append(
                pltpu.make_async_remote_copy(
                    src_ref=send.at[phase, peers[d - 1]],
                    dst_ref=arrive.at[phase, d - 1],
                    send_sem=send_sems.at[phase, d - 1],
                    recv_sem=recv_sems.at[phase, d - 1],
                    device_id={"tp": peers[d - 1]},
                    device_id_type=pl.DeviceIdType.MESH,
                )
            )
            copies[-1].start()
        total = unpack(send[phase, me])
        for d in range(1, n):
            copies[d - 1].wait_recv()
            total = total + unpack(arrive[phase, d - 1])
        return total, copies

    def gather_start(buffer, sent, received):
        copies = []
        for d in range(1, n):
            copies.append(
                pltpu.make_async_remote_copy(
                    src_ref=buffer.at[me],
                    dst_ref=buffer.at[me],
                    send_sem=sent.at[d - 1],
                    recv_sem=received.at[d - 1],
                    device_id={"tp": peers[d - 1]},
                    device_id_type=pl.DeviceIdType.MESH,
                )
            )
            copies[-1].start()
        return copies

    def gather_rows(phase, buffer):
        copies = gather_start(buffer, gather_send_sems.at[phase], gather_recv_sems.at[phase])
        for copy in copies:
            copy.wait_recv()
        return copies

    def pass_across():
        copy = pltpu.make_async_remote_copy(
            src_ref=passed,
            dst_ref=passed_to,
            send_sem=pass_sems.at[0],
            recv_sem=pass_sems.at[1],
            device_id={"section": 1 - section},
            device_id_type=pl.DeviceIdType.MESH,
        )
        copy.start()
        return copy

    def both(values, table, function):
        return jnp.concatenate(
            [
                function(values[:image_rows], table[0]),
                function(values[image_rows:], table[1]),
            ],
            axis=0,
        )

    loads[0].wait()
    loads[1].wait()
    product(attended[:all_images], attended[all_images:], out_i, out_t)
    pl.semaphore_wait(barrier, n)
    total, pending = scatter_sum(0)
    first[...] = shard[...] + both(total, mod, lambda rows, table: table[2:3] * rows)
    gather[me] = pack(
        both(first[...], mod, lambda rows, table: row_norm(rows, table[3:4], table[4:5]))
    )
    pending += gather_rows(0, gather)
    text_parts = []
    for j in range(n):
        block = unpack(gather[j])
        normed_i[j * image_rows : (j + 1) * image_rows] = block[:image_rows].astype(jnp.bfloat16)
        text_parts.append(block[image_rows:])
    normed_t[...] = jnp.concatenate(text_parts, axis=0).astype(jnp.bfloat16)
    loads[2].wait()
    loads[3].wait()

    @pl.loop(0, up_i.shape[1] // step)
    def _(index):
        columns = pl.ds(pl.multiple_of(index * step, step), step)
        for normed, up, hidden in ((normed_i, up_i, hidden_i), (normed_t, up_t, hidden_t)):
            hidden[:, columns] = jax.nn.gelu(
                jnp.dot(normed[...], up[:, columns], preferred_element_type=jnp.float32),
                approximate=True,
            ).astype(jnp.bfloat16)

    loads[4].wait()
    loads[5].wait()
    product(hidden_i[...], hidden_t[...], down_i, down_t)
    total, more = scatter_sum(1)
    pending += more
    made = (first[...] + both(total, mod, lambda rows, table: table[5:6] * rows)).astype(
        jnp.bfloat16
    )
    if last:
        rows_a = earlier[...].astype(jnp.float32)
        rows_b = jnp.where(
            section == 0, other[...].astype(jnp.float32), made.astype(jnp.float32)
        )
        next_gather[me] = jnp.concatenate(
            [rows_a[image_rows:], rows_b[image_rows:]], axis=0
        ).astype(jnp.bfloat16)
        text_copies = gather_start(next_gather, gather_send_sems.at[1], gather_recv_sems.at[1])
        normed = jnp.concatenate(
            [
                row_norm(rows[:image_rows], mod_last[r, 0:1], mod_last[r, 1:2])
                for r, rows in enumerate((rows_a, rows_b))
            ],
            axis=0,
        ).astype(jnp.bfloat16)
        velocity = jnp.dot(normed, final[...], preferred_element_type=jnp.float32)
        passed[...] = velocity
        copy = pass_across()
        copy.wait_recv()
        velocity_gather[me] = jnp.where(section == 0, passed_to[...], velocity)
        velocity_copies = gather_start(velocity_gather, velocity_send_sems, velocity_recv_sems)
        for waiting in text_copies + velocity_copies:
            waiting.wait_recv()
        pending += [copy] + text_copies + velocity_copies
        text_all[...] = next_gather[...]
        velocity_all[...] = velocity_gather[...]
    else:
        new_shard[...] = made
        passed[...] = pack(made.astype(jnp.float32))
        copy = pass_across()
        copy.wait_recv()
        pending.append(copy)
        next_shard[...] = jnp.where(section == 0, following[...], unpack(passed_to[...]))
        next_gather[me] = pack(
            both(
                next_shard[...],
                mod_following,
                lambda rows, table: row_norm(rows, table[0:1], table[1:2]),
            )
        )
        pending += gather_rows(1, next_gather)
        text_parts = []
        for j in range(n):
            block = unpack(next_gather[j])
            next_normed[j * image_rows : (j + 1) * image_rows] = block[:image_rows].astype(
                jnp.bfloat16
            )
            text_parts.append(block[image_rows:])
        next_normed[all_images:] = jnp.concatenate(text_parts, axis=0).astype(jnp.bfloat16)
    for copy in pending:
        copy.wait_send()


def finish(n, attended, shard, mod, rest, weights):
    last = len(rest) == 4
    rows, width = attended.shape[0], shard.shape[1]
    shard_rows = shard.shape[0]
    image_rows = shard_rows * 4 // 5
    hidden_width = weights[2].shape[1]
    vmem = pl.BlockSpec(memory_space=pltpu.VMEM)
    anywhere = pl.BlockSpec(memory_space=pl.ANY)
    block = (2 * shard_rows, width // 2)
    bf16, f32 = jnp.bfloat16, jnp.float32
    operands = [attended, shard, mod] + list(rest)
    image_total = 2 * image_rows
    text_total = 2 * (shard_rows - image_rows)
    if last:
        lanes = rest[3].shape[1]
        out_shape = [
            jax.ShapeDtypeStruct((n, text_total, width), bf16),
            jax.ShapeDtypeStruct((n, image_total, lanes), f32),
        ]
    else:
        out_shape = [
            jax.ShapeDtypeStruct((shard_rows, width), bf16),
            jax.ShapeDtypeStruct((rows, width), bf16),
            jax.ShapeDtypeStruct((shard_rows, width), f32),
        ]
    images = image_rows * n
    texts = rows - images
    scratch = [pltpu.VMEM(weight.shape, bf16) for weight in weights]
    scratch += [
        pltpu.VMEM((rows, width), f32),
        pltpu.VMEM((shard_rows, width), f32),
        pltpu.VMEM((2, n) + block, bf16),
        pltpu.VMEM((2, n - 1) + block, bf16),
        pltpu.VMEM((n,) + block, bf16),
        pltpu.VMEM((images, width), bf16),
        pltpu.VMEM((texts, width), bf16),
        pltpu.VMEM((images, hidden_width), bf16),
        pltpu.VMEM((texts, hidden_width), bf16),
        pltpu.SemaphoreType.DMA((6,)),
    ]
    scratch += [pltpu.SemaphoreType.DMA((2, n - 1))] * 4
    if last:
        scratch += [
            pltpu.VMEM((image_total, lanes), f32),
            pltpu.VMEM((image_total, lanes), f32),
            pltpu.SemaphoreType.DMA((2,)),
            pltpu.VMEM((n, text_total, width), bf16),
            pltpu.VMEM((n, image_total, lanes), f32),
            pltpu.SemaphoreType.DMA((n - 1,)),
            pltpu.SemaphoreType.DMA((n - 1,)),
        ]
    else:
        scratch += [
            pltpu.VMEM(block, bf16),
            pltpu.VMEM(block, bf16),
            pltpu.SemaphoreType.DMA((2,)),
            pltpu.VMEM((n,) + block, bf16),
        ]
    return pl.pallas_call(
        functools.partial(finish_kernel, n, image_rows, shard_rows - image_rows, last),
        out_shape=out_shape,
        in_specs=[vmem] * len(operands) + [anywhere] * 6,
        out_specs=[vmem] * len(out_shape),
        scratch_shapes=scratch,
        compiler_params=pltpu.CompilerParams(
            collective_id=1 if last else 0,
            has_side_effects=True,
            vmem_limit_bytes=48 * 1024 * 1024,
        ),
    )(*operands, *weights)


def attention_kernel(request, queries, fresh, stale, query_rank, key_info, attended):
    width = attended.shape[1]
    rows = attended.shape[0]
    rank, live = key_info[0, 0:1], key_info[0, 1:2]
    newer = rank <= query_rank[...]
    kept = jnp.broadcast_to(live > 0.0, newer.shape)
    fresh_bias = jnp.where(newer & kept, 0.0, NEGATIVE)
    stale_bias = jnp.where(jnp.logical_not(newer) & kept, 0.0, NEGATIVE)
    lane = lax.broadcasted_iota(jnp.int32, (rows, 128), 1)
    contract = (((1,), (1,)), ((), ()))
    for first in range(0, width, 128):
        keys = slice(first, first + 128)
        values = slice(width + first, width + first + 128)
        pair = queries[:, keys]
        made = []
        for part in range(2):
            own = (lane >= part * HD) & (lane < (part + 1) * HD)
            query = jnp.where(own, pair.astype(jnp.float32), 0.0).astype(jnp.bfloat16)
            fresh_scores = lax.dot_general(
                query, fresh[:, keys], contract, preferred_element_type=jnp.float32
            ) * HD ** (-0.5) + fresh_bias
            stale_scores = lax.dot_general(
                query, stale[0, :, keys], contract, preferred_element_type=jnp.float32
            ) * HD ** (-0.5) + stale_bias
            rowmax = jnp.maximum(
                jnp.max(fresh_scores, axis=-1, keepdims=True),
                jnp.max(stale_scores, axis=-1, keepdims=True),
            )
            fresh_exp = jnp.exp(fresh_scores - rowmax)
            stale_exp = jnp.exp(stale_scores - rowmax)
            totals = jnp.sum(fresh_exp, axis=-1, keepdims=True) + jnp.sum(
                stale_exp, axis=-1, keepdims=True
            )
            summed = jnp.dot(
                fresh_exp.astype(jnp.bfloat16),
                fresh[:, values],
                preferred_element_type=jnp.float32,
            ) + jnp.dot(
                stale_exp.astype(jnp.bfloat16),
                stale[0, :, values],
                preferred_element_type=jnp.float32,
            )
            made.append(summed / totals)
        attended[:, keys] = jnp.where(lane < HD, made[0], made[1]).astype(jnp.bfloat16)


def attention(request, mixed, fresh, stale, query_rank, key_info):
    rows, width = mixed.shape[0], mixed.shape[1] // 3
    keys = fresh.shape[0]
    whole = lambda shape: pl.BlockSpec(shape, lambda i, r: (0,) * len(shape))
    chosen = lambda shape: pl.BlockSpec((1,) + shape, lambda i, r: (r[0], 0, 0))
    return pl.pallas_call(
        attention_kernel,
        out_shape=jax.ShapeDtypeStruct((rows, width), jnp.bfloat16),
        grid_spec=pltpu.PrefetchScalarGridSpec(
            num_scalar_prefetch=1,
            grid=(1,),
            in_specs=[
                whole((rows, width)),
                whole((keys, 2 * width)),
                chosen((keys, 2 * width)),
                whole((rows, 1)),
                chosen((2, keys)),
            ],
            out_specs=whole((rows, width)),
        ),
        compiler_params=pltpu.CompilerParams(vmem_limit_bytes=40 * 1024 * 1024),
    )(request[None], mixed, fresh, stale, query_rank, key_info)


def sigma_of(index_value):
    progress = 1.0 - index_value / STEPS
    return TIME_SHIFT * progress / (1.0 + (TIME_SHIFT - 1.0) * progress)


def attend(queries, keys, values, allowed):
    heads = queries.shape[1] // HD
    split = lambda rows: rows.reshape(rows.shape[0], heads, HD)
    scores = jnp.einsum(
        "qhe,khe->hqk", split(queries), split(keys), preferred_element_type=jnp.float32
    ) * HD ** (-0.5)
    scores = jnp.where(allowed[None], scores, NEGATIVE)
    rowmax = jnp.max(scores, axis=-1, keepdims=True)
    exponent = jnp.where(allowed[None], jnp.exp(scores - rowmax), 0.0)
    totals = jnp.sum(exponent, axis=-1)
    summed = jnp.einsum(
        "hqk,khe->hqe",
        exponent.astype(jnp.bfloat16),
        split(values),
        preferred_element_type=jnp.float32,
    )
    result = summed / totals[..., None]
    return jnp.transpose(result, (1, 0, 2)).reshape(queries.shape).astype(jnp.bfloat16)


def ranks_of(patch_order, image_local, text_local):
    slot_count = patch_order.shape[0]
    order = jnp.arange(slot_count, dtype=jnp.int32)
    rank = jnp.sum(
        jnp.where(patch_order[:, None] == order[None, :], order[:, None], 0), axis=0
    )
    return jnp.concatenate(
        [
            jnp.repeat(rank, image_local // slot_count),
            jnp.repeat(order, text_local // slot_count),
        ]
    )


def kept_keys(live, image_local, text_local, seq_count):
    return jnp.concatenate(
        [
            jnp.ones((live.shape[0], seq_count, image_local), jnp.bool_),
            live.reshape(live.shape[0], seq_count, text_local),
        ],
        axis=2,
    ).reshape(live.shape[0], -1)


def allowed_keys(local, kept, seq_count):
    fresh = jnp.tile(local, seq_count)[None, :] <= local[:, None]
    kept = kept[:, None, :]
    return jnp.concatenate([fresh[None] & kept, ~fresh[None] & kept], axis=2)


def on_device(
    hidden_image,
    hidden_text,
    latent,
    timestep,
    text_length,
    text_keep,
    patch_order,
    stale_image_kv,
    stale_text_kv,
    mod_image,
    mod_text,
    mod_final,
    qkv_image,
    out_image,
    up_image,
    down_image,
    qkv_text,
    out_text,
    up_text,
    down_text,
    final_weight,
):
    requests, image_local, model_width = hidden_image.shape
    text_local = hidden_text.shape[1]
    local_width = qkv_image.shape[3]
    seq_count = lax.axis_size("seq")
    section_index = lax.axis_index("section")
    first_section = section_index == 0
    text_total = text_keep.shape[1]
    positions = jnp.arange(text_total, dtype=jnp.int32)
    live = (positions[None, :] < text_length[:, None]) & (text_keep == 1)
    local_rank = ranks_of(patch_order, image_local, text_local)
    kept = kept_keys(live, image_local, text_local, seq_count)
    stale_local = jnp.concatenate(
        [
            stale_image_kv[0].reshape(requests, image_local, 2 * local_width),
            stale_text_kv[0].reshape(requests, text_local, 2 * local_width),
        ],
        axis=1,
    )
    stale = lax.all_gather(stale_local, "seq", axis=1, tiled=True)
    tp_size = lax.axis_size("tp")
    shapes_fit = (
        image_local == 4 * text_local
        and text_local % (8 * tp_size) == 0
        and local_width % 128 == 0
        and requests == 2
        and latent.shape[2] <= 128
    )
    if shapes_fit:
        tp_count = lax.axis_size("tp")
        qkv_i = qkv_image[0].reshape(model_width, -1)
        qkv_t = qkv_text[0].reshape(model_width, -1)
        tp_index = lax.axis_index("tp")
        image_shard, text_shard = image_local // tp_count, text_local // tp_count
        shards = jnp.concatenate(
            [
                lax.dynamic_slice_in_dim(hidden_image, tp_index * image_shard, image_shard, 1),
                lax.dynamic_slice_in_dim(hidden_text, tp_index * text_shard, text_shard, 1),
            ],
            axis=1,
        ).astype(jnp.float32)
        mods = jnp.stack([mod_image[0], mod_text[0]], axis=1)
        weights = [
            value[0] for value in (out_image, out_text, up_image, up_text, down_image, down_text)
        ]
        dot = lambda left, right: jnp.dot(left, right, preferred_element_type=jnp.float32)

        def picker(moment):
            request = jnp.clip(moment - section_index, 0, requests - 1)
            return lambda values: lax.dynamic_index_in_dim(values, request, 0, keepdims=False)

        shard = shards[0]
        mod = mods[0]
        normed = jnp.concatenate(
            [
                row_norm(hidden_image[0].astype(jnp.float32), mod[0, 0], mod[0, 1]),
                row_norm(hidden_text[0].astype(jnp.float32), mod[1, 0], mod[1, 1]),
            ],
            axis=0,
        ).astype(jnp.bfloat16)
        query_rank = local_rank.astype(jnp.float32)[:, None]
        key_rank = jnp.tile(local_rank, seq_count).astype(jnp.float32)
        key_info = jnp.stack(
            [jnp.broadcast_to(key_rank, kept.shape), kept.astype(jnp.float32)], axis=1
        )
        lanes = 128
        final_lanes = jnp.pad(
            final_weight, ((0, 0), (0, lanes - final_weight.shape[1]))
        )
        made_rows, made_kv = [], []
        for moment in range(requests + 1):
            request = jnp.clip(moment - section_index, 0, requests - 1)
            mixed = jnp.concatenate(
                [dot(normed[:image_local], qkv_i), dot(normed[image_local:], qkv_t)], axis=0
            ).astype(jnp.bfloat16)
            fresh_local = mixed[:, local_width:]
            fresh = lax.all_gather(fresh_local, "seq", axis=0, tiled=True)
            attended = attention(request, mixed, fresh, stale, query_rank, key_info)
            made_kv.append(fresh_local)
            if moment < requests:
                following = picker(moment + 1)
                new_rows, normed, next_shard = finish(
                    tp_count, attended, shard, mod, (following(shards), following(mods)), weights
                )
                shard, mod = next_shard, following(mods)
                made_rows.append(new_rows)
            else:
                earlier = jnp.where(first_section, made_rows[0], made_rows[1])
                text_all, velocity_all = finish(
                    tp_count,
                    attended,
                    shard,
                    mod,
                    (earlier, made_rows[1], mod_final, final_lanes),
                    weights,
                )
        kv_out = jnp.stack(
            [jnp.where(first_section, made_kv[r], made_kv[r + 1]) for r in range(requests)]
        )
        regroup = lambda values, rows: jnp.swapaxes(
            values.reshape(tp_count, requests, rows, -1), 0, 1
        ).reshape(requests, tp_count * rows, -1)
        text_out = regroup(text_all, text_shard)
        velocity_used = regroup(velocity_all, image_shard)[:, :, : latent.shape[2]]
    else:
        allowed = allowed_keys(local_rank, kept, seq_count)
        qkv_i = qkv_image[0].reshape(model_width, -1)
        qkv_t = qkv_text[0].reshape(model_width, -1)
        inputs = jnp.concatenate([hidden_image, hidden_text], axis=1)
        arrived = None
        made_rows, made_kv = [], []
        for moment in range(requests + 1):
            request = jnp.clip(moment - section_index, 0, requests - 1)
            pick = lambda values: lax.dynamic_index_in_dim(values, request, 0, keepdims=False)
            rows = inputs[0] if moment == 0 else jnp.where(first_section, pick(inputs), arrived)
            mi, mt = pick(mod_image[0]), pick(mod_text[0])
            image_rows = rows[:image_local].astype(jnp.float32)
            text_rows = rows[image_local:].astype(jnp.float32)
            norm_i = row_norm(image_rows, mi[0], mi[1]).astype(jnp.bfloat16)
            norm_t = row_norm(text_rows, mt[0], mt[1]).astype(jnp.bfloat16)
            dot = lambda left, right: jnp.dot(left, right, preferred_element_type=jnp.float32)
            mixed = jnp.concatenate([dot(norm_i, qkv_i), dot(norm_t, qkv_t)], axis=0).astype(
                jnp.bfloat16
            )
            queries, fresh_local = mixed[:, :local_width], mixed[:, local_width:]
            fresh = lax.all_gather(fresh_local, "seq", axis=0, tiled=True)
            both = jnp.concatenate([fresh, pick(stale)], axis=0)
            attended = attend(
                queries, both[:, :local_width], both[:, local_width:], pick(allowed)
            )
            part = jnp.concatenate(
                [dot(attended[:image_local], out_image[0]), dot(attended[image_local:], out_text[0])],
                axis=0,
            )
            summed = lax.psum(part.astype(jnp.bfloat16), "tp").astype(jnp.float32)
            image_first = image_rows + mi[2] * summed[:image_local]
            text_first = text_rows + mt[2] * summed[image_local:]
            norm_i = row_norm(image_first, mi[3], mi[4]).astype(jnp.bfloat16)
            norm_t = row_norm(text_first, mt[3], mt[4]).astype(jnp.bfloat16)
            act = lambda values: jax.nn.gelu(values, approximate=True).astype(jnp.bfloat16)
            part = jnp.concatenate(
                [
                    dot(act(dot(norm_i, up_image[0])), down_image[0]),
                    dot(act(dot(norm_t, up_text[0])), down_text[0]),
                ],
                axis=0,
            )
            summed = lax.psum(part.astype(jnp.bfloat16), "tp").astype(jnp.float32)
            new_rows = jnp.concatenate(
                [image_first + mi[5] * summed[:image_local], text_first + mt[5] * summed[image_local:]],
                axis=0,
            ).astype(jnp.bfloat16)
            made_rows.append(new_rows)
            made_kv.append(fresh_local)
            if moment < requests:
                arrived = lax.ppermute(new_rows, "section", [(0, 1)])
        choose = lambda made: jnp.stack(
            [jnp.where(first_section, made[r], made[r + 1]) for r in range(requests)]
        )
        rows_out, kv_out = choose(made_rows), choose(made_kv)
        final_normed = row_norm(
            rows_out[:, :image_local].astype(jnp.float32), mod_final[:, :1], mod_final[:, 1:]
        ).astype(jnp.bfloat16)
        velocity = jnp.dot(
            final_normed.reshape(-1, model_width), final_weight, preferred_element_type=jnp.float32
        ).reshape(requests, image_local, -1)
        returned = lax.ppermute(velocity.astype(jnp.bfloat16), "section", [(1, 0)])
        velocity_used = jnp.where(first_section, returned.astype(velocity.dtype), velocity)
        text_out = rows_out[:, image_local:]
    index_value = timestep.astype(jnp.float32)
    sigma_now = sigma_of(index_value)
    sigma_next = sigma_of(index_value + 1.0)
    stepped = latent + (sigma_next - sigma_now)[:, None, None] * velocity_used
    denoised = latent - sigma_now[:, None, None] * velocity_used
    latent_part = jnp.where(first_section, stepped, denoised)[None]
    return (
        latent_part,
        kv_out[:, :image_local].reshape(requests, image_local, 2, local_width)[None],
        kv_out[:, image_local:].reshape(requests, text_local, 2, local_width)[None],
        text_out[None],
    )


def solution(mesh):
    in_specs = (
        P(None, "seq", None),
        P(None, "seq", None),
        P(None, "seq", None),
        P(),
        P(),
        P(),
        P(),
        P("section", None, "seq", None, "tp"),
        P("section", None, "seq", None, "tp"),
        P("section", None, None, None),
        P("section", None, None, None),
        P(),
        P("section", None, None, "tp"),
        P("section", "tp", None),
        P("section", None, "tp"),
        P("section", "tp", None),
        P("section", None, None, "tp"),
        P("section", "tp", None),
        P("section", None, "tp"),
        P("section", "tp", None),
        P(),
    )
    out_specs = (
        P("section", None, "seq", None),
        P("section", None, "seq", None, "tp"),
        P("section", None, "seq", None, "tp"),
        P("section", None, "seq", None),
    )
    return jax.shard_map(
        on_device, mesh=mesh, in_specs=in_specs, out_specs=out_specs, check_vma=False
    )
```

```python
import functools

import jax
import jax.numpy as jnp
from jax import lax
from jax.experimental import pallas as pl
from jax.experimental.pallas import tpu as pltpu
from jax.sharding import PartitionSpec as P

HD = 64
STEPS = 28


EPSILON = 1e-06
NEGATIVE = -1e30
TIME_SHIFT = 3.0


def row_norm(values, shift_rows, scale_rows):
    mean_value = jnp.mean(values, axis=-1, keepdims=True)
    centred = values - mean_value
    variance = jnp.mean(centred * centred, axis=-1, keepdims=True)
    return centred * lax.rsqrt(variance + EPSILON) * (1.0 + scale_rows) + shift_rows


def pack(values):
    half = values.shape[1] // 2
    return jnp.concatenate([values[:, :half], values[:, half:]], axis=0).astype(jnp.bfloat16)


def unpack(block):
    wide = block.astype(jnp.float32)
    rows = wide.shape[0] // 2
    return jnp.concatenate([wide[:rows], wide[rows:]], axis=1)


def finish_kernel(n, image_rows, text_rows, last, *refs):
    refs = list(refs)
    take = lambda count: [refs.pop(0) for _ in range(count)]
    attended, shard, mod = take(3)
    if last:
        earlier, other, mod_last, final = take(4)
    else:
        following, mod_following = take(2)
    weights = take(6)
    if last:
        text_all, velocity_all = take(2)
    else:
        new_shard, next_normed, next_shard = take(3)
    held = take(6)
    part, first, send, arrive, gather, normed_i, normed_t, hidden_i, hidden_t, weight_sems = take(10)
    send_sems, recv_sems, gather_send_sems, gather_recv_sems = take(4)
    passed, passed_to, pass_sems, next_gather = take(4)
    if last:
        velocity_gather, velocity_send_sems, velocity_recv_sems = take(3)
    me = lax.axis_index("tp")
    section = lax.axis_index("section")
    loads = [
        pltpu.make_async_copy(weights[i], held[i], weight_sems.at[i]) for i in range(6)
    ]
    for load in loads:
        load.start()
    peers = [lax.rem(me + d, n) for d in range(1, n)]
    barrier = pltpu.get_barrier_semaphore()
    for peer in peers:
        pl.semaphore_signal(
            barrier, inc=1, device_id={"tp": peer}, device_id_type=pl.DeviceIdType.MESH
        )
    pl.semaphore_signal(
        barrier,
        inc=1,
        device_id={"section": 1 - section},
        device_id_type=pl.DeviceIdType.MESH,
    )
    out_i, out_t, up_i, up_t, down_i, down_t = held
    width = shard.shape[1]
    step = min(512, width)
    all_images = image_rows * n

    def product(left_i, left_t, right_i, right_t):
        @pl.loop(0, width // step)
        def _(index):
            columns = pl.ds(pl.multiple_of(index * step, step), step)
            part[:all_images, columns] = jnp.dot(
                left_i, right_i[:, columns], preferred_element_type=jnp.float32
            )
            part[all_images:, columns] = jnp.dot(
                left_t, right_t[:, columns], preferred_element_type=jnp.float32
            )

    def scatter_sum(phase):
        for j in range(n):
            send[phase, j] = pack(
                jnp.concatenate(
                    [
                        part[j * image_rows : (j + 1) * image_rows],
                        part[all_images + j * text_rows : all_images + (j + 1) * text_rows],
                    ],
                    axis=0,
                )
            )
        copies = []
        for d in range(1, n):
            copies.append(
                pltpu.make_async_remote_copy(
                    src_ref=send.at[phase, peers[d - 1]],
                    dst_ref=arrive.at[phase, d - 1],
                    send_sem=send_sems.at[phase, d - 1],
                    recv_sem=recv_sems.at[phase, d - 1],
                    device_id={"tp": peers[d - 1]},
                    device_id_type=pl.DeviceIdType.MESH,
                )
            )
            copies[-1].start()
        total = unpack(send[phase, me])
        for d in range(1, n):
            copies[d - 1].wait_recv()
            total = total + unpack(arrive[phase, d - 1])
        return total, copies

    def gather_start(buffer, sent, received):
        copies = []
        for d in range(1, n):
            copies.append(
                pltpu.make_async_remote_copy(
                    src_ref=buffer.at[me],
                    dst_ref=buffer.at[me],
                    send_sem=sent.at[d - 1],
                    recv_sem=received.at[d - 1],
                    device_id={"tp": peers[d - 1]},
                    device_id_type=pl.DeviceIdType.MESH,
                )
            )
            copies[-1].start()
        return copies

    def gather_rows(phase, buffer):
        copies = gather_start(buffer, gather_send_sems.at[phase], gather_recv_sems.at[phase])
        for copy in copies:
            copy.wait_recv()
        return copies

    def pass_across():
        copy = pltpu.make_async_remote_copy(
            src_ref=passed,
            dst_ref=passed_to,
            send_sem=pass_sems.at[0],
            recv_sem=pass_sems.at[1],
            device_id={"section": 1 - section},
            device_id_type=pl.DeviceIdType.MESH,
        )
        copy.start()
        return copy

    def both(values, table, function):
        return jnp.concatenate(
            [
                function(values[:image_rows], table[0]),
                function(values[image_rows:], table[1]),
            ],
            axis=0,
        )

    loads[0].wait()
    loads[1].wait()
    product(attended[:all_images], attended[all_images:], out_i, out_t)
    pl.semaphore_wait(barrier, n)
    total, pending = scatter_sum(0)
    first[...] = shard[...] + both(total, mod, lambda rows, table: table[2:3] * rows)
    gather[me] = pack(
        both(first[...], mod, lambda rows, table: row_norm(rows, table[3:4], table[4:5]))
    )
    pending += gather_rows(0, gather)
    text_parts = []
    for j in range(n):
        block = unpack(gather[j])
        normed_i[j * image_rows : (j + 1) * image_rows] = block[:image_rows].astype(jnp.bfloat16)
        text_parts.append(block[image_rows:])
    normed_t[...] = jnp.concatenate(text_parts, axis=0).astype(jnp.bfloat16)
    loads[2].wait()
    loads[3].wait()

    @pl.loop(0, up_i.shape[1] // step)
    def _(index):
        columns = pl.ds(pl.multiple_of(index * step, step), step)
        for normed, up, hidden in ((normed_i, up_i, hidden_i), (normed_t, up_t, hidden_t)):
            hidden[:, columns] = jax.nn.gelu(
                jnp.dot(normed[...], up[:, columns], preferred_element_type=jnp.float32),
                approximate=True,
            ).astype(jnp.bfloat16)

    loads[4].wait()
    loads[5].wait()
    product(hidden_i[...], hidden_t[...], down_i, down_t)
    total, more = scatter_sum(1)
    pending += more
    made = (first[...] + both(total, mod, lambda rows, table: table[5:6] * rows)).astype(
        jnp.bfloat16
    )
    if last:
        rows_a = earlier[...].astype(jnp.float32)
        rows_b = jnp.where(
            section == 0, other[...].astype(jnp.float32), made.astype(jnp.float32)
        )
        next_gather[me] = jnp.concatenate(
            [rows_a[image_rows:], rows_b[image_rows:]], axis=0
        ).astype(jnp.bfloat16)
        text_copies = gather_start(next_gather, gather_send_sems.at[1], gather_recv_sems.at[1])
        normed = jnp.concatenate(
            [
                row_norm(rows[:image_rows], mod_last[r, 0:1], mod_last[r, 1:2])
                for r, rows in enumerate((rows_a, rows_b))
            ],
            axis=0,
        ).astype(jnp.bfloat16)
        velocity = jnp.dot(normed, final[...], preferred_element_type=jnp.float32)
        passed[...] = velocity
        copy = pass_across()
        copy.wait_recv()
        velocity_gather[me] = jnp.where(section == 0, passed_to[...], velocity)
        velocity_copies = gather_start(velocity_gather, velocity_send_sems, velocity_recv_sems)
        for waiting in text_copies + velocity_copies:
            waiting.wait_recv()
        pending += [copy] + text_copies + velocity_copies
        text_all[...] = next_gather[...]
        velocity_all[...] = velocity_gather[...]
    else:
        new_shard[...] = made
        passed[...] = pack(made.astype(jnp.float32))
        copy = pass_across()
        copy.wait_recv()
        pending.append(copy)
        next_shard[...] = jnp.where(section == 0, following[...], unpack(passed_to[...]))
        next_gather[me] = pack(
            both(
                next_shard[...],
                mod_following,
                lambda rows, table: row_norm(rows, table[0:1], table[1:2]),
            )
        )
        pending += gather_rows(1, next_gather)
        text_parts = []
        for j in range(n):
            block = unpack(next_gather[j])
            next_normed[j * image_rows : (j + 1) * image_rows] = block[:image_rows].astype(
                jnp.bfloat16
            )
            text_parts.append(block[image_rows:])
        next_normed[all_images:] = jnp.concatenate(text_parts, axis=0).astype(jnp.bfloat16)
    for copy in pending:
        copy.wait_send()


def finish(n, attended, shard, mod, rest, weights):
    last = len(rest) == 4
    rows, width = attended.shape[0], shard.shape[1]
    shard_rows = shard.shape[0]
    image_rows = shard_rows * 4 // 5
    hidden_width = weights[2].shape[1]
    vmem = pl.BlockSpec(memory_space=pltpu.VMEM)
    anywhere = pl.BlockSpec(memory_space=pl.ANY)
    block = (2 * shard_rows, width // 2)
    bf16, f32 = jnp.bfloat16, jnp.float32
    operands = [attended, shard, mod] + list(rest)
    image_total = 2 * image_rows
    text_total = 2 * (shard_rows - image_rows)
    if last:
        lanes = rest[3].shape[1]
        out_shape = [
            jax.ShapeDtypeStruct((n, text_total, width), bf16),
            jax.ShapeDtypeStruct((n, image_total, lanes), f32),
        ]
    else:
        out_shape = [
            jax.ShapeDtypeStruct((shard_rows, width), bf16),
            jax.ShapeDtypeStruct((rows, width), bf16),
            jax.ShapeDtypeStruct((shard_rows, width), f32),
        ]
    images = image_rows * n
    texts = rows - images
    scratch = [pltpu.VMEM(weight.shape, bf16) for weight in weights]
    scratch += [
        pltpu.VMEM((rows, width), f32),
        pltpu.VMEM((shard_rows, width), f32),
        pltpu.VMEM((2, n) + block, bf16),
        pltpu.VMEM((2, n - 1) + block, bf16),
        pltpu.VMEM((n,) + block, bf16),
        pltpu.VMEM((images, width), bf16),
        pltpu.VMEM((texts, width), bf16),
        pltpu.VMEM((images, hidden_width), bf16),
        pltpu.VMEM((texts, hidden_width), bf16),
        pltpu.SemaphoreType.DMA((6,)),
    ]
    scratch += [pltpu.SemaphoreType.DMA((2, n - 1))] * 4
    if last:
        scratch += [
            pltpu.VMEM((image_total, lanes), f32),
            pltpu.VMEM((image_total, lanes), f32),
            pltpu.SemaphoreType.DMA((2,)),
            pltpu.VMEM((n, text_total, width), bf16),
            pltpu.VMEM((n, image_total, lanes), f32),
            pltpu.SemaphoreType.DMA((n - 1,)),
            pltpu.SemaphoreType.DMA((n - 1,)),
        ]
    else:
        scratch += [
            pltpu.VMEM(block, bf16),
            pltpu.VMEM(block, bf16),
            pltpu.SemaphoreType.DMA((2,)),
            pltpu.VMEM((n,) + block, bf16),
        ]
    return pl.pallas_call(
        functools.partial(finish_kernel, n, image_rows, shard_rows - image_rows, last),
        out_shape=out_shape,
        in_specs=[vmem] * len(operands) + [anywhere] * 6,
        out_specs=[vmem] * len(out_shape),
        scratch_shapes=scratch,
        compiler_params=pltpu.CompilerParams(
            collective_id=1 if last else 0,
            has_side_effects=True,
            vmem_limit_bytes=48 * 1024 * 1024,
        ),
    )(*operands, *weights)


def front_kernel(moment, all_images, *refs):
    normed, weight_i, weight_t, stale, query_rank, key_info = refs[:6]
    attended, own_kv = refs[6:8]
    held_i, held_t, queries, fresh, weight_sems, send_sems, recv_sems = refs[8:]
    rows, width = attended.shape
    me = lax.axis_index("seq")
    count = fresh.shape[0]
    sibling = me + 1 - 2 * lax.rem(me, 2)
    across = lax.rem(me + 2, count)
    request = jnp.clip(moment - lax.axis_index("section"), 0, stale.shape[0] - 1)
    order = (1, 2, 0)
    loads = []
    for j in order:
        for stream, (weight, held) in enumerate(((weight_i, held_i), (weight_t, held_t))):
            loads.append(
                pltpu.make_async_copy(weight.at[j], held.at[j], weight_sems.at[stream, j])
            )
            loads[-1].start()
    barrier = pltpu.get_barrier_semaphore()
    for peer in (sibling, across):
        pl.semaphore_signal(
            barrier, inc=1, device_id={"seq": peer}, device_id_type=pl.DeviceIdType.MESH
        )

    def projected(index):
        loads[2 * index].wait()
        loads[2 * index + 1].wait()
        j = order[index]
        return jnp.concatenate(
            [
                jnp.dot(normed[:all_images], held_i[j], preferred_element_type=jnp.float32),
                jnp.dot(normed[all_images:], held_t[j], preferred_element_type=jnp.float32),
            ],
            axis=0,
        ).astype(jnp.bfloat16)

    def sending(slot, peer, index):
        return pltpu.make_async_remote_copy(
            src_ref=fresh.at[slot],
            dst_ref=fresh.at[slot],
            send_sem=send_sems.at[index],
            recv_sem=recv_sems.at[index],
            device_id={"seq": peer},
            device_id_type=pl.DeviceIdType.MESH,
        )

    for part in range(2):
        block = projected(part)
        own_kv[:, part * width : (part + 1) * width] = block
        fresh[me, :, part * width : (part + 1) * width] = block
    pl.semaphore_wait(barrier, 2)
    over_y = sending(me, across, 0)
    over_y.start()
    over_core = sending(me, sibling, 1)
    over_core.start()
    queries[...] = projected(2)
    rank, live = key_info[request, 0:1], key_info[request, 1:2]
    newer = rank <= query_rank[...]
    kept = jnp.broadcast_to(live > 0.0, newer.shape)
    fresh_bias = jnp.where(newer & kept, 0.0, NEGATIVE)
    stale_bias = jnp.where(jnp.logical_not(newer) & kept, 0.0, NEGATIVE)
    over_y.wait_recv()
    forward = sending(across, sibling, 2)
    forward.start()
    over_core.wait_recv()
    forward.wait_recv()
    lane = lax.broadcasted_iota(jnp.int32, (rows, 128), 1)
    contract = (((1,), (1,)), ((), ()))
    for first in range(0, width, 128):
        keys = slice(first, first + 128)
        values = slice(width + first, width + first + 128)
        pair = queries[:, keys]
        fresh_keys = fresh[:, :, keys].reshape(-1, 128)
        fresh_values = fresh[:, :, values].reshape(-1, 128)
        made = []
        for part in range(2):
            own = (lane >= part * HD) & (lane < (part + 1) * HD)
            query = jnp.where(own, pair.astype(jnp.float32), 0.0).astype(jnp.bfloat16)
            fresh_scores = lax.dot_general(
                query, fresh_keys, contract, preferred_element_type=jnp.float32
            ) * HD ** (-0.5) + fresh_bias
            stale_scores = lax.dot_general(
                query, stale[request, :, keys], contract, preferred_element_type=jnp.float32
            ) * HD ** (-0.5) + stale_bias
            rowmax = jnp.maximum(
                jnp.max(fresh_scores, axis=-1, keepdims=True),
                jnp.max(stale_scores, axis=-1, keepdims=True),
            )
            fresh_exp = jnp.exp(fresh_scores - rowmax)
            stale_exp = jnp.exp(stale_scores - rowmax)
            totals = jnp.sum(fresh_exp, axis=-1, keepdims=True) + jnp.sum(
                stale_exp, axis=-1, keepdims=True
            )
            summed = jnp.dot(
                fresh_exp.astype(jnp.bfloat16),
                fresh_values,
                preferred_element_type=jnp.float32,
            ) + jnp.dot(
                stale_exp.astype(jnp.bfloat16),
                stale[request, :, values],
                preferred_element_type=jnp.float32,
            )
            made.append(summed / totals)
        attended[:, keys] = jnp.where(lane < HD, made[0], made[1]).astype(jnp.bfloat16)
    for copy in (over_y, over_core, forward):
        copy.wait_send()


def front(moment, seq_count, all_images, normed, weight_i, weight_t, stale, query_rank, key_info):
    rows, width = normed.shape[0], weight_i.shape[2]
    vmem = pl.BlockSpec(memory_space=pltpu.VMEM)
    anywhere = pl.BlockSpec(memory_space=pl.ANY)
    bf16 = jnp.bfloat16
    return pl.pallas_call(
        functools.partial(front_kernel, moment, all_images),
        out_shape=[
            jax.ShapeDtypeStruct((rows, width), bf16),
            jax.ShapeDtypeStruct((rows, 2 * width), bf16),
        ],
        in_specs=[vmem, anywhere, anywhere, vmem, vmem, vmem],
        out_specs=[vmem, vmem],
        scratch_shapes=[
            pltpu.VMEM(weight_i.shape, bf16),
            pltpu.VMEM(weight_t.shape, bf16),
            pltpu.VMEM((rows, width), bf16),
            pltpu.VMEM((seq_count, rows, 2 * width), bf16),
            pltpu.SemaphoreType.DMA((2, 3)),
            pltpu.SemaphoreType.DMA((3,)),
            pltpu.SemaphoreType.DMA((3,)),
        ],
        compiler_params=pltpu.CompilerParams(
            collective_id=2 + moment,
            has_side_effects=True,
            vmem_limit_bytes=40 * 1024 * 1024,
        ),
    )(normed, weight_i, weight_t, stale, query_rank, key_info)


def sigma_of(index_value):
    progress = 1.0 - index_value / STEPS
    return TIME_SHIFT * progress / (1.0 + (TIME_SHIFT - 1.0) * progress)


def attend(queries, keys, values, allowed):
    heads = queries.shape[1] // HD
    split = lambda rows: rows.reshape(rows.shape[0], heads, HD)
    scores = jnp.einsum(
        "qhe,khe->hqk", split(queries), split(keys), preferred_element_type=jnp.float32
    ) * HD ** (-0.5)
    scores = jnp.where(allowed[None], scores, NEGATIVE)
    rowmax = jnp.max(scores, axis=-1, keepdims=True)
    exponent = jnp.where(allowed[None], jnp.exp(scores - rowmax), 0.0)
    totals = jnp.sum(exponent, axis=-1)
    summed = jnp.einsum(
        "hqk,khe->hqe",
        exponent.astype(jnp.bfloat16),
        split(values),
        preferred_element_type=jnp.float32,
    )
    result = summed / totals[..., None]
    return jnp.transpose(result, (1, 0, 2)).reshape(queries.shape).astype(jnp.bfloat16)


def ranks_of(patch_order, image_local, text_local):
    slot_count = patch_order.shape[0]
    order = jnp.arange(slot_count, dtype=jnp.int32)
    rank = jnp.sum(
        jnp.where(patch_order[:, None] == order[None, :], order[:, None], 0), axis=0
    )
    return jnp.concatenate(
        [
            jnp.repeat(rank, image_local // slot_count),
            jnp.repeat(order, text_local // slot_count),
        ]
    )


def kept_keys(live, image_local, text_local, seq_count):
    return jnp.concatenate(
        [
            jnp.ones((live.shape[0], seq_count, image_local), jnp.bool_),
            live.reshape(live.shape[0], seq_count, text_local),
        ],
        axis=2,
    ).reshape(live.shape[0], -1)


def allowed_keys(local, kept, seq_count):
    fresh = jnp.tile(local, seq_count)[None, :] <= local[:, None]
    kept = kept[:, None, :]
    return jnp.concatenate([fresh[None] & kept, ~fresh[None] & kept], axis=2)


def on_device(
    hidden_image,
    hidden_text,
    latent,
    timestep,
    text_length,
    text_keep,
    patch_order,
    stale_image_kv,
    stale_text_kv,
    mod_image,
    mod_text,
    mod_final,
    qkv_image,
    out_image,
    up_image,
    down_image,
    qkv_text,
    out_text,
    up_text,
    down_text,
    final_weight,
):
    requests, image_local, model_width = hidden_image.shape
    text_local = hidden_text.shape[1]
    local_width = qkv_image.shape[3]
    seq_count = lax.axis_size("seq")
    section_index = lax.axis_index("section")
    first_section = section_index == 0
    text_total = text_keep.shape[1]
    positions = jnp.arange(text_total, dtype=jnp.int32)
    live = (positions[None, :] < text_length[:, None]) & (text_keep == 1)
    local_rank = ranks_of(patch_order, image_local, text_local)
    kept = kept_keys(live, image_local, text_local, seq_count)
    stale_local = jnp.concatenate(
        [
            stale_image_kv[0].reshape(requests, image_local, 2 * local_width),
            stale_text_kv[0].reshape(requests, text_local, 2 * local_width),
        ],
        axis=1,
    )
    stale = lax.all_gather(stale_local, "seq", axis=1, tiled=True)
    tp_size = lax.axis_size("tp")
    shapes_fit = (
        image_local == 4 * text_local
        and text_local % (8 * tp_size) == 0
        and local_width % 128 == 0
        and requests == 2
        and seq_count == 4
        and latent.shape[2] <= 128
    )
    if shapes_fit:
        tp_count = lax.axis_size("tp")
        qkv_i = jnp.swapaxes(qkv_image[0], 0, 1)
        qkv_t = jnp.swapaxes(qkv_text[0], 0, 1)
        tp_index = lax.axis_index("tp")
        image_shard, text_shard = image_local // tp_count, text_local // tp_count
        shards = jnp.concatenate(
            [
                lax.dynamic_slice_in_dim(hidden_image, tp_index * image_shard, image_shard, 1),
                lax.dynamic_slice_in_dim(hidden_text, tp_index * text_shard, text_shard, 1),
            ],
            axis=1,
        ).astype(jnp.float32)
        mods = jnp.stack([mod_image[0], mod_text[0]], axis=1)
        weights = [
            value[0] for value in (out_image, out_text, up_image, up_text, down_image, down_text)
        ]
        dot = lambda left, right: jnp.dot(left, right, preferred_element_type=jnp.float32)

        def picker(moment):
            request = jnp.clip(moment - section_index, 0, requests - 1)
            return lambda values: lax.dynamic_index_in_dim(values, request, 0, keepdims=False)

        shard = shards[0]
        mod = mods[0]
        normed = jnp.concatenate(
            [
                row_norm(hidden_image[0].astype(jnp.float32), mod[0, 0], mod[0, 1]),
                row_norm(hidden_text[0].astype(jnp.float32), mod[1, 0], mod[1, 1]),
            ],
            axis=0,
        ).astype(jnp.bfloat16)
        query_rank = local_rank.astype(jnp.float32)[:, None]
        key_rank = jnp.tile(local_rank, seq_count).astype(jnp.float32)
        key_info = jnp.stack(
            [jnp.broadcast_to(key_rank, kept.shape), kept.astype(jnp.float32)], axis=1
        )
        lanes = 128
        final_lanes = jnp.pad(
            final_weight, ((0, 0), (0, lanes - final_weight.shape[1]))
        )
        made_rows, made_kv = [], []
        for moment in range(requests + 1):
            attended, fresh_local = front(
                moment, seq_count, image_local, normed, qkv_i, qkv_t, stale, query_rank, key_info
            )
            made_kv.append(fresh_local)
            if moment < requests:
                following = picker(moment + 1)
                new_rows, normed, next_shard = finish(
                    tp_count, attended, shard, mod, (following(shards), following(mods)), weights
                )
                shard, mod = next_shard, following(mods)
                made_rows.append(new_rows)
            else:
                earlier = jnp.where(first_section, made_rows[0], made_rows[1])
                text_all, velocity_all = finish(
                    tp_count,
                    attended,
                    shard,
                    mod,
                    (earlier, made_rows[1], mod_final, final_lanes),
                    weights,
                )
        kv_out = jnp.stack(
            [jnp.where(first_section, made_kv[r], made_kv[r + 1]) for r in range(requests)]
        )
        regroup = lambda values, rows: jnp.swapaxes(
            values.reshape(tp_count, requests, rows, -1), 0, 1
        ).reshape(requests, tp_count * rows, -1)
        text_out = regroup(text_all, text_shard)
        velocity_used = regroup(velocity_all, image_shard)[:, :, : latent.shape[2]]
    else:
        allowed = allowed_keys(local_rank, kept, seq_count)
        qkv_i = qkv_image[0].reshape(model_width, -1)
        qkv_t = qkv_text[0].reshape(model_width, -1)
        inputs = jnp.concatenate([hidden_image, hidden_text], axis=1)
        arrived = None
        made_rows, made_kv = [], []
        for moment in range(requests + 1):
            request = jnp.clip(moment - section_index, 0, requests - 1)
            pick = lambda values: lax.dynamic_index_in_dim(values, request, 0, keepdims=False)
            rows = inputs[0] if moment == 0 else jnp.where(first_section, pick(inputs), arrived)
            mi, mt = pick(mod_image[0]), pick(mod_text[0])
            image_rows = rows[:image_local].astype(jnp.float32)
            text_rows = rows[image_local:].astype(jnp.float32)
            norm_i = row_norm(image_rows, mi[0], mi[1]).astype(jnp.bfloat16)
            norm_t = row_norm(text_rows, mt[0], mt[1]).astype(jnp.bfloat16)
            dot = lambda left, right: jnp.dot(left, right, preferred_element_type=jnp.float32)
            mixed = jnp.concatenate([dot(norm_i, qkv_i), dot(norm_t, qkv_t)], axis=0).astype(
                jnp.bfloat16
            )
            queries, fresh_local = mixed[:, :local_width], mixed[:, local_width:]
            fresh = lax.all_gather(fresh_local, "seq", axis=0, tiled=True)
            both = jnp.concatenate([fresh, pick(stale)], axis=0)
            attended = attend(
                queries, both[:, :local_width], both[:, local_width:], pick(allowed)
            )
            part = jnp.concatenate(
                [dot(attended[:image_local], out_image[0]), dot(attended[image_local:], out_text[0])],
                axis=0,
            )
            summed = lax.psum(part.astype(jnp.bfloat16), "tp").astype(jnp.float32)
            image_first = image_rows + mi[2] * summed[:image_local]
            text_first = text_rows + mt[2] * summed[image_local:]
            norm_i = row_norm(image_first, mi[3], mi[4]).astype(jnp.bfloat16)
            norm_t = row_norm(text_first, mt[3], mt[4]).astype(jnp.bfloat16)
            act = lambda values: jax.nn.gelu(values, approximate=True).astype(jnp.bfloat16)
            part = jnp.concatenate(
                [
                    dot(act(dot(norm_i, up_image[0])), down_image[0]),
                    dot(act(dot(norm_t, up_text[0])), down_text[0]),
                ],
                axis=0,
            )
            summed = lax.psum(part.astype(jnp.bfloat16), "tp").astype(jnp.float32)
            new_rows = jnp.concatenate(
                [image_first + mi[5] * summed[:image_local], text_first + mt[5] * summed[image_local:]],
                axis=0,
            ).astype(jnp.bfloat16)
            made_rows.append(new_rows)
            made_kv.append(fresh_local)
            if moment < requests:
                arrived = lax.ppermute(new_rows, "section", [(0, 1)])
        choose = lambda made: jnp.stack(
            [jnp.where(first_section, made[r], made[r + 1]) for r in range(requests)]
        )
        rows_out, kv_out = choose(made_rows), choose(made_kv)
        final_normed = row_norm(
            rows_out[:, :image_local].astype(jnp.float32), mod_final[:, :1], mod_final[:, 1:]
        ).astype(jnp.bfloat16)
        velocity = jnp.dot(
            final_normed.reshape(-1, model_width), final_weight, preferred_element_type=jnp.float32
        ).reshape(requests, image_local, -1)
        returned = lax.ppermute(velocity.astype(jnp.bfloat16), "section", [(1, 0)])
        velocity_used = jnp.where(first_section, returned.astype(velocity.dtype), velocity)
        text_out = rows_out[:, image_local:]
    index_value = timestep.astype(jnp.float32)
    sigma_now = sigma_of(index_value)
    sigma_next = sigma_of(index_value + 1.0)
    stepped = latent + (sigma_next - sigma_now)[:, None, None] * velocity_used
    denoised = latent - sigma_now[:, None, None] * velocity_used
    latent_part = jnp.where(first_section, stepped, denoised)[None]
    return (
        latent_part,
        kv_out[:, :image_local].reshape(requests, image_local, 2, local_width)[None],
        kv_out[:, image_local:].reshape(requests, text_local, 2, local_width)[None],
        text_out[None],
    )


def solution(mesh):
    in_specs = (
        P(None, "seq", None),
        P(None, "seq", None),
        P(None, "seq", None),
        P(),
        P(),
        P(),
        P(),
        P("section", None, "seq", None, "tp"),
        P("section", None, "seq", None, "tp"),
        P("section", None, None, None),
        P("section", None, None, None),
        P(),
        P("section", None, None, "tp"),
        P("section", "tp", None),
        P("section", None, "tp"),
        P("section", "tp", None),
        P("section", None, None, "tp"),
        P("section", "tp", None),
        P("section", None, "tp"),
        P("section", "tp", None),
        P(),
    )
    out_specs = (
        P("section", None, "seq", None),
        P("section", None, "seq", None, "tp"),
        P("section", None, "seq", None, "tp"),
        P("section", None, "seq", None),
    )
    return jax.shard_map(
        on_device, mesh=mesh, in_specs=in_specs, out_specs=out_specs, check_vma=False
    )
```
